256 devices in a mesh: section: 32 (over z, x), tensor: 8 (over y, core).
Axes of the slice: x: 4, y: 4, z: 8, core: 2. Of those that a mesh axis runs over, the one named last changes fastest.
Arguments:
- grad_in: bfloat16 [24576, 4096], P('section', 'tensor'), may hold values from -6 to 6
- layer_in: bfloat16 [24576, 4096], P('section', 'tensor'), may hold values from -6 to 6
- norm_gain: float32 [32, 4096], P('section', 'tensor'), may hold values from 0.5 to 1.5
- attn_weights: bfloat16 [32, 6, 32, 128, 128], P('section', None, 'tensor'), may hold values from 0 to 2, as said below
- attn_out: bfloat16 [24576, 4096], P('section', 'tensor'), may hold values from -6 to 6
- w_value: bfloat16 [131072, 1024], P(('section', 'tensor')), may hold values from -0.1875 to 0.1875
- w_out: bfloat16 [131072, 4096], P(('section', 'tensor')), may hold values from -0.09375 to 0.09375
- fac_out_in: bfloat16 [32, 32, 4096], P('section', None, 'tensor'), may hold values from -0.09375 to 0.09375
- fac_out_out: bfloat16 [32, 32, 4096], P('section', None, 'tensor'), may hold values from -0.09375 to 0.09375
- fac_val_in: bfloat16 [32, 32, 4096], P('section', None, 'tensor'), may hold values from -0.09375 to 0.09375
- fac_val_out: bfloat16 [32, 32, 1024], P('section', None, 'tensor'), may hold values from -0.1875 to 0.1875
- coef: float32 [32, 2, 16, 32, 32], P('section'), may hold values from -0.3125 to 0.3125
- eig: float32 [32, 2, 32, 32], P('section'), may hold values from 0.01 to 90, as said below
Outputs:
- grad_next: bfloat16 [24576, 4096], P('section', 'tensor')
- scores: float32 [24576, 16], P('section')
The draws below stay inside these ranges and needn't reach their ends.
Inputs may be any that keep to these rules, and one draw needn't show every extreme that they name: `attn_weights`: zero where the key comes after the query. `eig`: positive.
All inputs are finite; a program needn't handle non-finite values.
Results may differ from the reference program's by a relative error of at most 0.004.
Values may be sent and summed in bfloat16 or wider, within the bound.
A program may use at most 64 MiB of HBM per device.

```python
import math
import jax
import jax.numpy as jnp
from jax import lax

D = 4096
H = 32
KV = 8
HD = 128
Q = 16
E = 32
LEN = 128
SEQS = 6
S = 32
TOK = 768


def draw_attn_weights(key, part):
    key = jax.random.fold_in(key, 11)
    raw = jax.random.uniform(key, (S, SEQS, H, LEN, LEN), jnp.float32, 0.0, 2.0)
    row_pos = lax.broadcasted_iota(jnp.int32, (LEN, LEN), 0)
    col_pos = lax.broadcasted_iota(jnp.int32, (LEN, LEN), 1)
    keep = (col_pos <= row_pos).astype(jnp.float32)
    weight = keep / (row_pos.astype(jnp.float32) + 1.0)
    return (raw * weight).astype(jnp.bfloat16)


def draw_eig(key, part):
    key = jax.random.fold_in(key, 23)
    logs = jax.random.uniform(key, (S, 2, E, E), jnp.float32, math.log(0.01), math.log(10.0))
    depth = lax.broadcasted_iota(jnp.int32, (S, 2, E, E), 0).astype(jnp.float32) / max(S - 1, 1)
    rising = jnp.exp(depth * math.log(3.0))
    return jnp.exp(logs) * rising


def shard_levels(stream_key, extent, cuts, least, top_value):
    factor_of, own = 1.0, jax.random.fold_in(stream_key, 6)
    for axis_at, parts in cuts:
        steps = jnp.exp(jax.random.uniform(jax.random.fold_in(own, axis_at), (parts,), jnp.float32, least / len(cuts), top_value / len(cuts)))
        factor_of = factor_of * jnp.repeat(steps, extent[axis_at] // parts).reshape([-1 if axis == axis_at else 1 for axis in range(len(extent))])
    return factor_of


def scatter_about(rng, extent, spread, reach, split=(), dtype=jnp.bfloat16):
    drawn = spread * jax.random.normal(rng, extent, jnp.float32)
    if split:
        drawn = drawn * shard_levels(rng, extent, split, -0.22, 0.18)
    return jnp.clip(drawn, -reach, reach).astype(dtype)


def setup_inputs(seed: int = 0) -> dict:
    seeds = jax.random.split(jax.random.key(seed), 14)
    grad_in = scatter_about(seeds[0], (S * TOK, D), 1.0, 6.0, ((0, 32), (1, 8)))
    layer_in = scatter_about(seeds[1], (S * TOK, D), 1.0, 6.0, ((0, 32), (1, 8)))
    norm_gain = jnp.clip(1.0 + 0.1 * jax.random.normal(seeds[2], (S, D), jnp.float32), 0.5, 1.5)
    attn_weights = draw_attn_weights(jax.random.fold_in(seeds[13], 71), 0)
    attn_out = scatter_about(seeds[4], (S * TOK, H * HD), 1.0, 6.0, ((0, 32), (1, 8)))
    w_value = scatter_about(seeds[5], (S * D, KV * HD), (KV * HD) ** -0.5, 0.1875, ((0, 256),))
    w_out = scatter_about(seeds[6], (S * H * HD, D), D ** -0.5, 0.09375, ((0, 256),))
    fac_out_in = scatter_about(seeds[7], (S, E, H * HD), (H * HD) ** -0.5, 0.09375, ((0, 32), (2, 8)))
    fac_out_out = scatter_about(seeds[8], (S, E, D), D ** -0.5, 0.09375, ((0, 32), (2, 8)))
    fac_val_in = scatter_about(seeds[9], (S, E, D), D ** -0.5, 0.09375, ((0, 32), (2, 8)))
    fac_val_out = scatter_about(seeds[10], (S, E, KV * HD), (KV * HD) ** -0.5, 0.1875, ((0, 32), (2, 8)))
    coef = scatter_about(seeds[11], (S, 2, Q, E, E), 0.02, 0.3125, ((0, 32),), jnp.float32)
    eig = draw_eig(jax.random.fold_in(seeds[13], 71), 0)
    return {"grad_in": grad_in, "layer_in": layer_in, "norm_gain": norm_gain, "attn_weights": attn_weights, "attn_out": attn_out, "w_value": w_value, "w_out": w_out, "fac_out_in": fac_out_in, "fac_out_out": fac_out_out, "fac_val_in": fac_val_in, "fac_val_out": fac_val_out, "coef": coef, "eig": eig}


def section_pass(items):
    dy, x, g, probs, att, wv, wo, uo, vo, uv, vv = items
    grp = H // KV
    d_att = jnp.dot(dy, wo.T, preferred_element_type=jnp.float32).astype(jnp.bfloat16)
    d_att5 = d_att.astype(jnp.float32).reshape(SEQS, LEN, KV, grp, HD)
    probs5 = probs.astype(jnp.float32).reshape(SEQS, KV, grp, LEN, LEN)
    d_val = jnp.einsum('bkgij,bikge->bjke', probs5, d_att5).reshape(TOK, KV * HD).astype(jnp.bfloat16)
    d_norm = jnp.dot(d_val, wv.T, preferred_element_type=jnp.float32)
    xf = x.astype(jnp.float32)
    inv = lax.rsqrt(lax.optimization_barrier(jnp.mean(xf * xf, axis=-1)) + 1e-05)
    cross = lax.optimization_barrier(jnp.mean(xf * g * d_norm, axis=-1))
    d_x = dy.astype(jnp.float32) + inv[:, None] * g * d_norm - xf * (inv ** 3 * cross)[:, None]
    scaled = (xf * g).astype(jnp.bfloat16)
    p_out = jnp.dot(att, uo.T, preferred_element_type=jnp.float32)
    s_out = jnp.dot(dy, vo.T, preferred_element_type=jnp.float32)
    p_val = inv[:, None] * jnp.dot(scaled, uv.T, preferred_element_type=jnp.float32)
    s_val = jnp.dot(d_val, vv.T, preferred_element_type=jnp.float32)
    return (d_x.astype(jnp.bfloat16), p_out, s_out, p_val, s_val)

def reference(grad_in, layer_in, norm_gain, attn_weights, attn_out, w_value, w_out, fac_out_in, fac_out_out, fac_val_in, fac_val_out, coef, eig):
    items = (grad_in.reshape(S, TOK, D), layer_in.reshape(S, TOK, D), norm_gain, attn_weights, attn_out.reshape(S, TOK, H * HD), w_value.reshape(S, D, KV * HD), w_out.reshape(S, H * HD, D), fac_out_in, fac_out_out, fac_val_in, fac_val_out)
    d_x, p_out, s_out, p_val, s_val = lax.map(section_pass, items)
    damp = 0.1 * jnp.mean(eig)
    kern = coef / (eig[:, :, None] + damp)
    hp = lax.Precision.HIGHEST
    left_o = jnp.einsum('sti,sqij->stqj', p_out, kern[:, 0], precision=hp)
    left_v = jnp.einsum('sti,sqij->stqj', p_val, kern[:, 1], precision=hp)
    score = jnp.einsum('stqj,stj->stq', left_o, s_out, precision=hp) + jnp.einsum('stqj,stj->stq', left_v, s_val, precision=hp)
    shifted = jnp.concatenate([d_x[1:], jnp.zeros((1, TOK, D), jnp.bfloat16)], axis=0)
    return (shifted.reshape(S * TOK, D), score.reshape(S * TOK, Q))
```

```python
import functools

import jax
import jax.numpy as jnp
from jax import lax
from jax.experimental import pallas as pl
from jax.experimental.pallas import tpu as pltpu
from jax.sharding import PartitionSpec as P

D = 4096
E = 32
Q = 16
SEQS = 6
LEN = 128
W = 512
HD = 128
T = 8
HALF = LEN // 2
MESH = pl.DeviceIdType.MESH
F32 = jnp.float32
BF16 = jnp.bfloat16
HIGH = lax.Precision.HIGHEST


def contract(left, right):
    return lax.dot_general(left, right, (((1,), (1,)), ((), ())), preferred_element_type=F32)


def lanes_folded(value):
    return value[:, 0:128] + value[:, 128:256] + value[:, 256:384] + value[:, 384:512]


def kernel(
    nsec,
    nx,
    dy_h,
    x_h,
    g_h,
    aw_h,
    ao_h,
    wv_h,
    wo_h,
    foi_h,
    foo_h,
    fvi_h,
    fvo_h,
    coef_h,
    eig_h,
    gn_h,
    sc_h,
    dyf,
    dvf,
    x_v,
    ao_v,
    aw_v,
    wv_v,
    wo_v,
    fo_v,
    fs_v,
    fp_v,
    fvof,
    g_v,
    coef_v,
    eig_v,
    du_v,
    dx_v,
    zero_v,
    p_part,
    p_sib,
    p_snd,
    p_rcv,
    sqt,
    rb,
    mb,
    eb1,
    eb2,
    wk,
    sc_v,
    lsem,
    dy_ss,
    dy_rs,
    dv_ss,
    dv_rs,
    m_ss,
    m_rs,
    sq_ss,
    sq_rs,
    fv_ss,
    fv_rs,
    e1_ss,
    e1_rs,
    e2_ss,
    e2_rs,
    ps_ss,
    ps_rs,
    pr_ss,
    pr_rs,
    sc_ss,
    sc_rs,
    dx_ss,
    dx_rs,
):
    nz = nsec // nx
    s = lax.axis_index("section")
    t = lax.axis_index("tensor")
    core = lax.rem(t, 2)
    chip = t // 2
    right = lax.rem(t + 2, T)
    left = lax.rem(t + 6, T)
    across = lax.rem(t + 4, T)
    sib = t + 1 - 2 * core
    sx = lax.rem(s, nx)
    sz = s // nx

    def remote(src, dst, ss, rs, **where):
        return pltpu.make_async_remote_copy(
            src_ref=src, dst_ref=dst, send_sem=ss, recv_sem=rs, device_id=where, device_id_type=MESH
        )

    loads = [
        pltpu.make_async_copy(dy_h, dyf.at[t], lsem.at[0]),
        pltpu.make_async_copy(ao_h, ao_v, lsem.at[1]),
        pltpu.make_async_copy(x_h, x_v, lsem.at[2]),
        pltpu.make_async_copy(g_h, g_v, lsem.at[3]),
        pltpu.make_async_copy(foi_h.at[0], fo_v.at[pl.ds(0, E)], lsem.at[4]),
        pltpu.make_async_copy(foo_h.at[0], fs_v.at[pl.ds(E, E)], lsem.at[5]),
        pltpu.make_async_copy(fvi_h.at[0], fp_v.at[pl.ds(2 * E, E)], lsem.at[6]),
        pltpu.make_async_copy(eig_h.at[0], eig_v, lsem.at[7]),
        pltpu.make_async_copy(wo_h, wo_v, lsem.at[8]),
        pltpu.make_async_copy(aw_h.at[0], aw_v, lsem.at[9]),
        pltpu.make_async_copy(wv_h, wv_v, lsem.at[10]),
        pltpu.make_async_copy(coef_h.at[0], coef_v, lsem.at[11]),
        pltpu.make_async_copy(fvo_h.at[0], fvof.at[t, pl.ds(E, E)], lsem.at[12]),
    ]

    fo_v[...] = jnp.zeros_like(fo_v)
    fs_v[...] = jnp.zeros_like(fs_v)
    fp_v[...] = jnp.zeros_like(fp_v)
    fvof[...] = jnp.zeros_like(fvof)
    wk[...] = jnp.zeros_like(wk)

    barrier = pltpu.get_barrier_semaphore()
    for d in range(1, T):
        pl.semaphore_signal(
            barrier, inc=1, device_id={"tensor": lax.rem(t + d, T)}, device_id_type=MESH
        )
    for d in range(1, nx):
        pl.semaphore_signal(
            barrier, inc=1, device_id={"section": sz * nx + lax.rem(sx + d, nx)}, device_id_type=MESH
        )
    for d in range(1, nz):
        pl.semaphore_signal(
            barrier, inc=1, device_id={"section": lax.rem(sz + d, nz) * nx + sx}, device_id_type=MESH
        )
    pl.semaphore_signal(
        barrier, inc=1, device_id={"section": lax.rem(s + 1, nsec)}, device_id_type=MESH
    )
    for load in loads:
        load.start()
    pl.semaphore_wait(barrier, (T - 1) + (nx - 1) + (nz - 1) + 1)

    def ring_copy(kind, b, buf, own, ss, rs):
        low, high, whole = pl.ds(0, HALF), pl.ds(HALF, HALF), pl.ds(0, LEN)
        source, rows, target = [
            (t, low, right),
            (t, high, right),
            (t, low, left),
            (t, high, left),
            (left, low, right),
            (right, high, left),
            (t, whole, sib),
            (left, whole, sib),
            (right, whole, sib),
            (across, low, sib),
            (across, high, sib),
        ][kind]
        src = buf.at[source, b, rows]
        if own is not None and kind in (0, 1, 2, 3, 6):
            src = own.at[b, rows]
        return remote(
            src, buf.at[source, b, rows], ss.at[kind, b], rs.at[kind, b], tensor=target
        )

    def dy_copy(kind, b):
        return ring_copy(kind, b, dyf, dy_h, dy_ss, dy_rs)

    def dv_copy(kind, b):
        return ring_copy(kind, b, dvf, None, dv_ss, dv_rs)

    def start_own(copy, b):
        for kind in (0, 3, 1, 2, 6):
            copy(kind, b).start()

    def pass_on(copy, b):
        copy(0, b).wait_recv()
        copy(4, b).start()
        copy(3, b).wait_recv()
        copy(5, b).start()

    def pass_sib(copy, b):
        copy(1, b).wait_recv()
        copy(7, b).start()
        copy(2, b).wait_recv()
        copy(8, b).start()

    def pass_across(copy, b):
        copy(4, b).wait_recv()
        copy(9, b).start()
        copy(5, b).wait_recv()
        copy(10, b).start()

    def wait_rest(copy, b):
        for kind in (6, 7, 8, 9, 10):
            copy(kind, b).wait_recv()

    def spread(src, dst, ss, rs, d):
        return remote(src, dst, ss, rs, tensor=lax.rem(t + d, T))

    def m_copy(b, d):
        return spread(mb.at[b, t], mb.at[b, t], m_ss.at[b, d], m_rs.at[b, d], d)

    def sq_copy(d):
        return spread(sqt.at[t], sqt.at[t], sq_ss.at[d], sq_rs.at[d], d)

    def fv_copy(d):
        return spread(
            fvo_h.at[0], fvof.at[t, pl.ds(E, E)], fv_ss.at[d], fv_rs.at[d], d
        )

    def sc_copy(d):
        return spread(
            sc_v, sc_h.at[:, pl.ds(t * 16, 16)], sc_ss.at[d], sc_rs.at[d], d
        )

    def e1_copy(d):
        return remote(
            eb1.at[sx],
            eb1.at[sx],
            e1_ss.at[d],
            e1_rs.at[d],
            section=sz * nx + lax.rem(sx + d, nx),
        )

    def e2_copy(d):
        return remote(
            eb2.at[sz],
            eb2.at[sz],
            e2_ss.at[d],
            e2_rs.at[d],
            section=lax.rem(sz + d, nz) * nx + sx,
        )

    def ps_copy():
        return remote(p_part.at[1 - core], p_sib, ps_ss, ps_rs, tensor=sib)

    def pr_copy(d):
        other = lax.rem(chip + d, 4)
        return remote(
            p_snd.at[other], p_rcv.at[chip], pr_ss.at[d], pr_rs.at[d], tensor=2 * other + core
        )

    def dx_copy(b):
        return remote(
            dx_v.at[b],
            gn_h.at[b],
            dx_ss.at[b],
            dx_rs.at[b],
            section=lax.rem(s + nsec - 1, nsec),
        )

    def zero_copy():
        return pltpu.make_async_copy(zero_v, gn_h, lsem.at[13])

    start_own(dy_copy, 0)
    start_own(dy_copy, 1)
    for d in range(1, T):
        fv_copy(d).start()

    @pl.when(s == nsec - 1)
    def _():
        zero_v[...] = jnp.zeros_like(zero_v)
        zero_copy().start()

    loads[7].wait()
    ev = eig_v[...]
    eb1[sx] = jnp.full((1, 128), jnp.sum(ev[0] + ev[1]), F32)
    for d in range(1, nx):
        e1_copy(d).start()

    for at in (0, 1, 2, 3, 4, 5, 6):
        loads[at].wait()

    def project(b, carry):
        xf = x_v[b].astype(F32)
        scaled = (xf * g_v[...]).astype(BF16)
        sums = jnp.sum(lanes_folded(xf * xf).T, axis=0, keepdims=True)
        sqt[t, b] = sums
        part = contract(ao_v[b], fo_v[...])
        part += contract(dyf[t, b], fs_v[...])
        part += contract(scaled, fp_v[...])
        part = part.reshape(4, 2, 16, 128)
        p_part[0, :, b] = part[:, 0]
        p_part[1, :, b] = part[:, 1]
        return carry

    lax.fori_loop(0, SEQS, project, 0)
    for d in range(1, T):
        sq_copy(d).start()
    ps_copy().start()
    for at in (8, 9, 10, 11, 12):
        loads[at].wait()

    def step(i, carry):
        @pl.when(i < SEQS)
        def _():
            pass_on(dy_copy, i)

        @pl.when(i + 2 < SEQS)
        def _():
            start_own(dy_copy, i + 2)

        @pl.when((i >= 1) & (i < SEQS + 1))
        def _():
            pass_on(dv_copy, i - 1)

        @pl.when(i < SEQS)
        def _():
            pass_sib(dy_copy, i)

        @pl.when((i >= 1) & (i < SEQS + 1))
        def _():
            pass_sib(dv_copy, i - 1)

        @pl.when((i >= 2) & (i < SEQS + 2))
        def _():
            b = i - 2
            wait_rest(dv_copy, b)
            vals = jnp.concatenate([dvf[k, b] for k in range(T)], axis=1)
            du = contract(vals, wv_v[...])
            du_v[b] = du
            cross = x_v[b].astype(F32) * g_v[...] * du
            mb[b, t] = jnp.sum(lanes_folded(cross).T, axis=0, keepdims=True)
            for d in range(1, T):
                m_copy(b, d).start()

        @pl.when(i >= 3)
        def _():
            b = i - 3
            for d in range(1, T):
                m_copy(b, d).wait_recv()
            total = mb[b, 0]
            for k in range(1, T):
                total += mb[b, k]
            mean = jnp.broadcast_to(total * (1.0 / D), (LEN, 128)).T
            inv = rb[b]
            cubed = inv * inv * inv * mean
            for k in range(4):
                cols = slice(k * 128, (k + 1) * 128)
                dx = (
                    dyf[t, b, :, cols].astype(F32)
                    + inv * g_v[:, cols] * du_v[b, :, cols]
                    - x_v[b, :, cols].astype(F32) * cubed
                )
                dx_v[b, :, cols] = dx.astype(BF16)

            @pl.when(s > 0)
            def _():
                dx_copy(b).start()

        @pl.when(i == 0)
        def _():
            ps_copy().wait_recv()
            p_snd[...] = p_part[core] + p_sib[...]
            for d in range(1, 4):
                pr_copy(d).start()
            for d in range(1, nx):
                e1_copy(d).wait_recv()
            eb2[sz] = jnp.sum(eb1[...], axis=0)
            for d in range(1, nz):
                e2_copy(d).start()

        @pl.when(i == 1)
        def _():
            for d in range(1, T):
                sq_copy(d).wait_recv()

            def turn(b, carry):
                total = sqt[0, b]
                for k in range(1, T):
                    total += sqt[k, b]
                inv = lax.rsqrt(total * (1.0 / D) + 1e-05)
                rb[b] = jnp.broadcast_to(inv, (LEN, 128)).T
                return carry

            lax.fori_loop(0, SEQS, turn, 0)

        @pl.when(i == 2)
        def _():
            for d in range(1, nz):
                e2_copy(d).wait_recv()
            damp = jnp.sum(eb2[...], axis=0) * (0.1 / (nsec * 2 * E * E))
            damp = damp[:, 0:E]
            for m in range(2):
                under = eig_v[m] + damp
                for q in range(Q):
                    wk[m * 2 * E : m * 2 * E + E, m * 1024 + q * E : m * 1024 + (q + 1) * E] = (
                        coef_v[m, q] / under
                    )
            row = lax.broadcasted_iota(jnp.int32, (E, W), 0)
            col = lax.broadcasted_iota(jnp.int32, (E, W), 1)
            wk[E : 2 * E, W : 2 * W] = (lax.rem(col, E) == row).astype(F32)

        @pl.when(i < SEQS)
        def _():
            pass_across(dy_copy, i)

        @pl.when((i >= 1) & (i < SEQS + 1))
        def _():
            pass_across(dv_copy, i - 1)

        @pl.when(i < SEQS)
        def _():
            wait_rest(dy_copy, i)
            acc = contract(dyf[0, i], wo_v[:, 0:W])
            for k in range(1, T):
                acc += contract(dyf[k, i], wo_v[:, k * W : (k + 1) * W])
            d_att = acc.astype(BF16)
            d_att = jnp.concatenate([d_att[:, h * HD : (h + 1) * HD] for h in range(4)], axis=0)
            probs = aw_v[i].reshape(4 * LEN, LEN)
            d_val = lax.dot_general(
                probs, d_att, (((0,), (0,)), ((), ())), preferred_element_type=F32
            )
            dvf[t, i] = d_val.astype(BF16)
            start_own(dv_copy, i)

        return carry

    lax.fori_loop(0, SEQS + 3, step, 0)

    for d in range(1, T):
        fv_copy(d).wait_recv()
    for d in range(1, 4):
        pr_copy(d).wait_recv()
    mine = pl.ds(t * 16, 16)
    proj = p_snd[chip]
    for d in range(1, 4):
        proj += p_rcv[lax.rem(chip + d, 4)]
    proj = proj.reshape(96, 128)
    inv = rb[:, mine, :].reshape(96, 128)
    vals = dvf[0, :, mine, :].reshape(96, 128)
    s_val = contract(vals, fvof[0])
    for k in range(1, T):
        s_val += contract(dvf[k, :, mine, :].reshape(96, 128), fvof[k])
    pick = wk[:, W : 2 * W]
    left_o = jnp.dot(proj, wk[:, 0:W], precision=HIGH, preferred_element_type=F32)
    left_v = jnp.dot(proj * inv, wk[:, 2 * W : 3 * W], precision=HIGH, preferred_element_type=F32)
    tiled_o = jnp.dot(proj, pick, precision=HIGH, preferred_element_type=F32)
    tiled_v = jnp.dot(s_val, pick, precision=HIGH, preferred_element_type=F32)
    both = left_o * tiled_o + left_v * tiled_v
    row = lax.broadcasted_iota(jnp.int32, (W, 128), 0)
    col = lax.broadcasted_iota(jnp.int32, (W, 128), 1)
    group = (row // E == col).astype(F32)
    scores = jnp.dot(both, group, precision=HIGH, preferred_element_type=F32)
    sc_v[...] = scores[:, 0:Q].reshape(SEQS, 16, Q)
    keep = pltpu.make_async_copy(sc_v, sc_h.at[:, mine], lsem.at[14])
    keep.start()
    for d in range(1, T):
        sc_copy(d).start()

    def drain(b, carry):
        for kind in range(11):
            dy_copy(kind, b).wait_send()
            dv_copy(kind, b).wait_send()
        for d in range(1, T):
            m_copy(b, d).wait_send()

        @pl.when(s > 0)
        def _():
            dx_copy(b).wait_send()

        @pl.when(s < nsec - 1)
        def _():
            dx_copy(b).wait_recv()

        return carry

    lax.fori_loop(0, SEQS, drain, 0)
    for d in range(1, T):
        sq_copy(d).wait_send()
        fv_copy(d).wait_send()
    for d in range(1, nx):
        e1_copy(d).wait_send()
    for d in range(1, nz):
        e2_copy(d).wait_send()
    ps_copy().wait_send()
    for d in range(1, 4):
        pr_copy(d).wait_send()

    @pl.when(s == nsec - 1)
    def _():
        zero_copy().wait()

    keep.wait()
    for d in range(1, T):
        sc_copy(d).wait()


def per_device(nsec, nx, *arrays):
    (dy, x, g, aw, ao, wv, wo, foi, foo, fvi, fvo, coef, eig) = arrays
    nz = nsec // nx
    blocks = (SEQS, LEN, W)
    dma = pltpu.SemaphoreType.DMA
    vmem = pltpu.VMEM
    anywhere = pl.BlockSpec(memory_space=pl.ANY)
    grad_next, scores = pl.pallas_call(
        functools.partial(kernel, nsec, nx),
        out_shape=(
            jax.ShapeDtypeStruct(blocks, BF16),
            jax.ShapeDtypeStruct((SEQS, LEN, Q), F32),
        ),
        in_specs=[anywhere] * 13,
        out_specs=(anywhere, anywhere),
        scratch_shapes=[
            vmem((T, *blocks), BF16),
            vmem((T, SEQS, LEN, HD), BF16),
            vmem(blocks, BF16),
            vmem(blocks, BF16),
            vmem((SEQS, 4, LEN, LEN), BF16),
            vmem((W, 2 * W), BF16),
            vmem((W, D), BF16),
            vmem((128, W), BF16),
            vmem((128, W), BF16),
            vmem((128, W), BF16),
            vmem((T, 128, HD), BF16),
            vmem((1, W), F32),
            vmem((2, Q, E, E), F32),
            vmem((2, E, E), F32),
            vmem(blocks, F32),
            vmem(blocks, BF16),
            vmem(blocks, BF16),
            vmem((2, 4, SEQS, 16, 128), F32),
            vmem((4, SEQS, 16, 128), F32),
            vmem((4, SEQS, 16, 128), F32),
            vmem((4, SEQS, 16, 128), F32),
            vmem((T, SEQS, 1, 128), F32),
            vmem((SEQS, LEN, 128), F32),
            vmem((SEQS, T, 1, 128), F32),
            vmem((nx, 1, 128), F32),
            vmem((nz, 1, 128), F32),
            vmem((128, 3 * W), F32),
            vmem((SEQS, 16, Q), F32),
            dma((15,)),
            dma((11, SEQS)),
            dma((11, SEQS)),
            dma((11, SEQS)),
            dma((11, SEQS)),
            dma((SEQS, T)),
            dma((SEQS, T)),
            dma((T,)),
            dma((T,)),
            dma((T,)),
            dma((T,)),
            dma((nx,)),
            dma((nx,)),
            dma((nz,)),
            dma((nz,)),
            dma,
            dma,
            dma((4,)),
            dma((4,)),
            dma((T,)),
            dma((T,)),
            dma((SEQS,)),
            dma((SEQS,)),
        ],
        compiler_params=pltpu.CompilerParams(
            collective_id=0, has_side_effects=True, vmem_limit_bytes=48 * 2**20
        ),
        cost_estimate=pl.CostEstimate(
            flops=8 * 10**9, bytes_accessed=10 * 2**20, transcendentals=0
        ),
    )(
        dy.reshape(blocks),
        x.reshape(blocks),
        g,
        aw,
        ao.reshape(blocks),
        wv,
        wo,
        foi,
        foo,
        fvi,
        fvo,
        coef,
        eig,
    )
    return grad_next.reshape(SEQS * LEN, W), scores.reshape(SEQS * LEN, Q)


def solution(mesh):
    nsec = mesh.shape["section"]
    nx = 4 if nsec >= 16 else 2
    placed = (
        P("section", "tensor"),
        P("section", "tensor"),
        P("section", "tensor"),
        P("section", None, "tensor", None, None),
        P("section", "tensor"),
        P(("section", "tensor"), None),
        P(("section", "tensor"), None),
        P("section", None, "tensor"),
        P("section", None, "tensor"),
        P("section", None, "tensor"),
        P("section", None, "tensor"),
        P("section", None, None, None, None),
        P("section", None, None, None),
    )
    return jax.shard_map(
        functools.partial(per_device, nsec, nx),
        mesh=mesh,
        in_specs=placed,
        out_specs=(P("section", "tensor"), P("section", None)),
        check_vma=False,
    )
```

```python
import functools

import jax
import jax.numpy as jnp
from jax import lax
from jax.experimental import pallas as pl
from jax.experimental.pallas import tpu as pltpu
from jax.sharding import PartitionSpec as P

D = 4096
E = 32
Q = 16
SEQS = 6
LEN = 128
W = 512
HD = 128
T = 8
HALF = LEN // 2
MESH = pl.DeviceIdType.MESH
LIMIT = 64_600_000
F32 = jnp.float32
BF16 = jnp.bfloat16
HIGH = lax.Precision.HIGHEST


def contract(left, right):
    return lax.dot_general(left, right, (((1,), (1,)), ((), ())), preferred_element_type=F32)


def lanes_folded(value):
    return value[:, 0:128] + value[:, 128:256] + value[:, 256:384] + value[:, 384:512]


def kernel(
    nsec,
    dy_h,
    x_h,
    g_h,
    aw_h,
    ao_h,
    wv_h,
    wo_h,
    foi_h,
    foo_h,
    fvi_h,
    fvo_h,
    coef_h,
    eig_h,
    gn_h,
    sc_h,
    dyf,
    dvf,
    x_v,
    ao_v,
    aw_v,
    wv_v,
    wo_v,
    fo_v,
    fs_v,
    fp_v,
    fvof,
    g_v,
    coef_v,
    eig_v,
    du_v,
    dx_v,
    p_part,
    p_sib,
    p_snd,
    p_rcv,
    sqt,
    rb,
    mb,
    ev,
    wk,
    sc_v,
    lsem,
    dy_ss,
    dy_rs,
    dv_ss,
    dv_rs,
    m_ss,
    m_rs,
    e_ss,
    e_rs,
    xs,
):
    phases = nsec.bit_length() - 1
    s = lax.axis_index("section")
    t = lax.axis_index("tensor")
    core = lax.rem(t, 2)
    chip = t // 2
    right = lax.rem(t + 2, T)
    left = lax.rem(t + 6, T)
    across = lax.rem(t + 4, T)
    sib = t + 1 - 2 * core

    def partner(phase):
        bit = lax.rem(s // 2**phase, 2)
        return s + 2**phase * (1 - 2 * bit)

    def remote(src, dst, ss, rs, **where):
        return pltpu.make_async_remote_copy(
            src_ref=src, dst_ref=dst, send_sem=ss, recv_sem=rs, device_id=where, device_id_type=MESH
        )

    loads = [
        pltpu.make_async_copy(dy_h, dyf.at[t], lsem.at[0]),
        pltpu.make_async_copy(ao_h, ao_v, lsem.at[1]),
        pltpu.make_async_copy(x_h, x_v, lsem.at[2]),
        pltpu.make_async_copy(g_h, g_v, lsem.at[3]),
        pltpu.make_async_copy(foi_h.at[0], fo_v.at[pl.ds(0, E)], lsem.at[4]),
        pltpu.make_async_copy(foo_h.at[0], fs_v.at[pl.ds(E, E)], lsem.at[5]),
        pltpu.make_async_copy(fvi_h.at[0], fp_v.at[pl.ds(2 * E, E)], lsem.at[6]),
        pltpu.make_async_copy(eig_h.at[0], eig_v, lsem.at[7]),
        pltpu.make_async_copy(wo_h, wo_v, lsem.at[8]),
        pltpu.make_async_copy(aw_h.at[0], aw_v, lsem.at[9]),
        pltpu.make_async_copy(wv_h, wv_v, lsem.at[10]),
        pltpu.make_async_copy(coef_h.at[0], coef_v, lsem.at[11]),
        pltpu.make_async_copy(fvo_h.at[0], fvof.at[t, pl.ds(E, E)], lsem.at[12]),
    ]

    fo_v[...] = jnp.zeros_like(fo_v)
    fs_v[...] = jnp.zeros_like(fs_v)
    fp_v[...] = jnp.zeros_like(fp_v)
    fvof[...] = jnp.zeros_like(fvof)

    barrier = pltpu.get_barrier_semaphore()
    for d in range(1, T):
        pl.semaphore_signal(
            barrier, inc=1, device_id={"tensor": lax.rem(t + d, T)}, device_id_type=MESH
        )
    for phase in range(phases):
        pl.semaphore_signal(
            barrier, inc=1, device_id={"section": partner(phase)}, device_id_type=MESH
        )
    pl.semaphore_signal(
        barrier, inc=1, device_id={"section": lax.rem(s + 1, nsec)}, device_id_type=MESH
    )
    for load in loads:
        load.start()
    pl.semaphore_wait(barrier, (T - 1) + phases + 1)

    low, high, whole = pl.ds(0, HALF), pl.ds(HALF, HALF), pl.ds(0, LEN)
    routes = [
        (t, low, right, 0),
        (t, high, left, 0),
        (t, high, right, 1),
        (t, low, left, 1),
        (left, low, right, 2),
        (right, high, left, 2),
        (t, whole, sib, 3),
        (left, whole, sib, 3),
        (right, whole, sib, 3),
        (across, low, sib, 3),
        (across, high, sib, 3),
    ]

    class Gather:
        def __init__(self, buf, own, ss, rs):
            self.buf, self.own, self.ss, self.rs = buf, own, ss, rs

        def send(self, b, *kinds):
            for kind in kinds:
                source, rows, target, group = routes[kind]
                dst = self.buf.at[source, b, rows]
                src = dst
                if self.own is not None and kind in (0, 1, 2, 3, 6):
                    src = self.own.at[b, rows]
                remote(src, dst, self.ss.at[b], self.rs.at[group, b], tensor=target).start()

        def arrived(self, b, group):
            blocks = self.buf.at[pl.ds(0, 4 if group == 3 else 1), b]
            remote(blocks, blocks, self.ss.at[b], self.rs.at[group, b], tensor=sib).wait_recv()

        def sent(self, b):
            blocks = self.buf.at[pl.ds(0, 7), b]
            remote(blocks, blocks, self.ss.at[b], self.rs.at[0, b], tensor=sib).wait_send()

    dy = Gather(dyf, dy_h, dy_ss, dy_rs)
    dv = Gather(dvf, None, dv_ss, dv_rs)
    own_kinds = (0, 1, 2, 3, 6)

    def to_peers(src, dst, ss, rs):
        for d in range(1, T):
            remote(src, dst, ss, rs, tensor=lax.rem(t + d, T)).start()

    def both(ref, ss, rs):
        return remote(ref, ref, ss, rs, tensor=sib)

    def e_copy(phase):
        return remote(
            ev.at[0], ev.at[1 + phase], e_ss.at[phase], e_rs.at[phase], section=partner(phase)
        )

    def ps_copy():
        return remote(p_part.at[1 - core], p_sib, xs.at[0], xs.at[1], tensor=sib)

    def dx_copy(b):
        return remote(
            dx_v.at[b], gn_h.at[b], xs.at[2], xs.at[3], section=lax.rem(s + nsec - 1, nsec)
        )

    def fold_eig(phase):
        e_copy(phase).wait()
        ev[0] = ev[0] + ev[1 + phase]

    dy.send(0, *own_kinds)
    dy.send(1, *own_kinds)

    loads[7].wait()
    ev[0] = jnp.full((1, 128), jnp.sum(eig_v[0] + eig_v[1]), F32)
    e_copy(0).start()

    for at in (0, 1, 2, 3, 4, 5, 6):
        loads[at].wait()

    def project(b, carry):
        xf = x_v[b].astype(F32)
        scaled = (xf * g_v[...]).astype(BF16)
        sqt[t, b] = jnp.sum(lanes_folded(xf * xf).T, axis=0, keepdims=True)
        part = contract(ao_v[b], fo_v[...])
        part += contract(dyf[t, b], fs_v[...])
        part += contract(scaled, fp_v[...])
        p_part[lax.rem(b, 2), b // 2] = part
        return carry

    lax.fori_loop(0, SEQS, project, 0)
    to_peers(sqt.at[t], sqt.at[t], xs.at[4], xs.at[5])
    ps_copy().start()

    def step(i, carry):
        @pl.when(i < SEQS)
        def _():
            dy.arrived(i, 0)
            dy.send(i, 4, 5)

        @pl.when(i + 2 < SEQS)
        def _():
            dy.send(i + 2, *own_kinds)

        @pl.when((i >= 1) & (i < SEQS + 1))
        def _():
            dy.arrived(i - 1, 2)
            dy.send(i - 1, 9, 10)

        @pl.when(i < SEQS)
        def _():
            dy.arrived(i, 1)
            dy.send(i, 7, 8)

        @pl.when((i >= 3) & (i < SEQS + 3))
        def _():
            dv.arrived(i - 3, 2)
            dv.send(i - 3, 9, 10)

        @pl.when((i >= 2) & (i < SEQS + 2))
        def _():
            dv.arrived(i - 2, 0)
            dv.send(i - 2, 4, 5)
            dv.arrived(i - 2, 1)
            dv.send(i - 2, 7, 8)

        @pl.when(i >= 4)
        def _():
            b = i - 4
            both(mb.at[b, pl.ds(0, T - 1)], m_ss.at[b], m_rs.at[b]).wait_recv()
            total = mb[b, 0]
            for k in range(1, T):
                total += mb[b, k]
            mean = jnp.broadcast_to(total * (1.0 / D), (LEN, 128)).T
            inv = rb[b]
            cubed = inv * inv * inv * mean
            for k in range(4):
                cols = slice(k * 128, (k + 1) * 128)
                dx = (
                    dyf[t, b, :, cols].astype(F32)
                    + inv * g_v[:, cols] * du_v[b, :, cols]
                    - x_v[b, :, cols].astype(F32) * cubed
                )
                dx_v[b, :, cols] = dx.astype(BF16)

            @pl.when(s > 0)
            def _():
                dx_copy(b).start()

        @pl.when((i >= 3) & (i < SEQS + 3))
        def _():
            b = i - 3
            dv.arrived(b, 3)
            vals = jnp.concatenate([dvf[k, b] for k in range(T)], axis=1)
            du = contract(vals, wv_v[...])
            du_v[b] = du
            cross = x_v[b].astype(F32) * g_v[...] * du
            mb[b, t] = jnp.sum(lanes_folded(cross).T, axis=0, keepdims=True)
            to_peers(mb.at[b, t], mb.at[b, t], m_ss.at[b], m_rs.at[b])

        for phase in range(phases):

            @pl.when(i == phase + 1)
            def _():
                fold_eig(phase)
                if phase + 1 < phases:
                    e_copy(phase + 1).start()

        @pl.when(i == 1)
        def _():
            for at in (8, 9, 10, 11, 12):
                loads[at].wait()
            ps_copy().wait_recv()
            for k in range(3):
                p_snd[k] = p_part[core, k] + p_sib[k]
            both(sqt.at[pl.ds(0, T - 1)], xs.at[4], xs.at[5]).wait_recv()

            def turn(b, carry):
                total = sqt[0, b]
                for k in range(1, T):
                    total += sqt[k, b]
                inv = lax.rsqrt(total * (1.0 / D) + 1e-05)
                rb[b] = jnp.broadcast_to(inv, (LEN, 128)).T
                return carry

            lax.fori_loop(0, SEQS, turn, 0)

        @pl.when(i == SEQS - 1)
        def _():
            to_peers(fvo_h.at[0], fvof.at[t, pl.ds(E, E)], xs.at[6], xs.at[7])
            for k in range(3):

                @pl.when(chip != k)
                def _():
                    slot = lax.rem(chip + 3 - k, 4)
                    remote(
                        p_snd.at[k], p_rcv.at[slot], xs.at[8], xs.at[9], tensor=2 * k + core
                    ).start()

        @pl.when((i >= 1) & (i < SEQS + 1))
        def _():
            b = i - 1
            dy.arrived(b, 3)
            acc = contract(dyf[0, b], wo_v[:, 0:W])
            for k in range(1, T):
                acc += contract(dyf[k, b], wo_v[:, k * W : (k + 1) * W])
            d_att = acc.astype(BF16)
            d_att = jnp.concatenate([d_att[:, h * HD : (h + 1) * HD] for h in range(4)], axis=0)
            probs = aw_v[b].reshape(4 * LEN, LEN)
            d_val = lax.dot_general(
                probs, d_att, (((0,), (0,)), ((), ())), preferred_element_type=F32
            )
            dvf[t, b] = d_val.astype(BF16)
            dv.send(b, *own_kinds)

        @pl.when(i == SEQS)
        def _():
            damp = ev[0] * (0.1 / (nsec * 2 * E * E))
            damp = damp[:, 0:E]
            wk[...] = jnp.zeros_like(wk)
            for m in range(2):
                under = eig_v[m] + damp
                for q in range(Q):
                    wk[m * 2 * E : m * 2 * E + E, m * 1024 + q * E : m * 1024 + (q + 1) * E] = (
                        coef_v[m, q] / under
                    )
            row = lax.broadcasted_iota(jnp.int32, (E, W), 0)
            col = lax.broadcasted_iota(jnp.int32, (E, W), 1)
            wk[E : 2 * E, W : 2 * W] = (lax.rem(col, E) == row).astype(F32)

        return carry

    lax.fori_loop(0, SEQS + 4, step, 0)

    both(fvof.at[pl.ds(0, T - 1), pl.ds(E, E)], xs.at[6], xs.at[7]).wait_recv()
    here = sc_h.at[:, pl.ds(pl.multiple_of(t * LEN, LEN), LEN)]
    keep = pltpu.make_async_copy(sc_v, here, lsem.at[14])

    @pl.when(t < SEQS)
    def _():
        both(p_rcv.at[pl.ds(0, 3)], xs.at[8], xs.at[9]).wait_recv()
        proj = p_snd[chip] + p_rcv[0] + p_rcv[1] + p_rcv[2]
        s_val = contract(dvf[0, t], fvof[0])
        for k in range(1, T):
            s_val += contract(dvf[k, t], fvof[k])
        pick = wk[:, W : 2 * W]

        def exact(left, right):
            return jnp.dot(left, right, precision=HIGH, preferred_element_type=F32)

        pairs = exact(proj, wk[:, 0:W]) * exact(proj, pick)
        pairs += exact(proj * rb[t], wk[:, 2 * W : 3 * W]) * exact(s_val, pick)
        row = lax.broadcasted_iota(jnp.int32, (Q, W), 0)
        col = lax.broadcasted_iota(jnp.int32, (Q, W), 1)
        group = (row == col // E).astype(F32)
        sc_v[...] = lax.dot_general(
            group, pairs, (((1,), (1,)), ((), ())), precision=HIGH, preferred_element_type=F32
        )
        keep.start()
        to_peers(sc_v, here, xs.at[10], xs.at[11])

    def drain(b, carry):
        dy.sent(b)
        dv.sent(b)
        both(mb.at[b, pl.ds(0, T - 1)], m_ss.at[b], m_rs.at[b]).wait_send()
        return carry

    lax.fori_loop(0, SEQS, drain, 0)
    both(sqt.at[pl.ds(0, T - 1)], xs.at[4], xs.at[5]).wait_send()
    both(fvof.at[pl.ds(0, T - 1), pl.ds(E, E)], xs.at[6], xs.at[7]).wait_send()
    ps_copy().wait_send()

    @pl.when(chip == 3)
    def _():
        both(p_snd.at[pl.ds(0, 3)], xs.at[8], xs.at[9]).wait_send()

    @pl.when(chip < 3)
    def _():
        both(p_snd.at[pl.ds(0, 2)], xs.at[8], xs.at[9]).wait_send()

    @pl.when(s > 0)
    def _():
        both(dx_v, xs.at[2], xs.at[3]).wait_send()

    @pl.when(s < nsec - 1)
    def _():
        both(gn_h, xs.at[2], xs.at[3]).wait_recv()

    @pl.when(s == nsec - 1)
    def _():
        dx_v[...] = jnp.zeros_like(dx_v)
        zero = pltpu.make_async_copy(dx_v, gn_h, lsem.at[13])
        zero.start()
        zero.wait()

    @pl.when(t < SEQS)
    def _():
        keep.wait()
        both(wk.at[pl.ds(0, Q), pl.ds(0, 7 * LEN)], xs.at[10], xs.at[11]).wait_send()
        both(sc_h.at[:, pl.ds(0, (SEQS - 1) * LEN)], xs.at[10], xs.at[11]).wait_recv()

    @pl.when(t >= SEQS)
    def _():
        both(sc_h, xs.at[10], xs.at[11]).wait_recv()


def per_device(nsec, *arrays):
    (dy, x, g, aw, ao, wv, wo, foi, foo, fvi, fvo, coef, eig) = arrays
    blocks = (SEQS, LEN, W)
    phases = nsec.bit_length() - 1
    dma = pltpu.SemaphoreType.DMA
    vmem = pltpu.VMEM
    grad_next, scores = pl.pallas_call(
        functools.partial(kernel, nsec),
        out_shape=(
            jax.ShapeDtypeStruct(blocks, BF16),
            jax.ShapeDtypeStruct((Q, SEQS * LEN), F32),
        ),
        in_specs=[pl.BlockSpec(memory_space=pltpu.HBM)] * 13,
        out_specs=(pl.BlockSpec(memory_space=pl.ANY), pl.BlockSpec(memory_space=pl.ANY)),
        scratch_shapes=[
            vmem((T, *blocks), BF16),
            vmem((T, SEQS, LEN, HD), BF16),
            vmem(blocks, BF16),
            vmem(blocks, BF16),
            vmem((SEQS, 4, LEN, LEN), BF16),
            vmem((W, 2 * W), BF16),
            vmem((W, D), BF16),
            vmem((128, W), BF16),
            vmem((128, W), BF16),
            vmem((128, W), BF16),
            vmem((T, 128, HD), BF16),
            vmem((1, W), F32),
            vmem((2, Q, E, E), F32),
            vmem((2, E, E), F32),
            vmem(blocks, F32),
            vmem(blocks, BF16),
            vmem((2, 3, LEN, 128), F32),
            vmem((3, LEN, 128), F32),
            vmem((3, LEN, 128), F32),
            vmem((3, LEN, 128), F32),
            vmem((T, SEQS, 1, 128), F32),
            vmem((SEQS, LEN, 128), F32),
            vmem((SEQS, T, 1, 128), F32),
            vmem((1 + phases, 1, 128), F32),
            vmem((128, 3 * W), F32),
            vmem((Q, LEN), F32),
            dma((15,)),
            dma((SEQS,)),
            dma((4, SEQS)),
            dma((SEQS,)),
            dma((4, SEQS)),
            dma((SEQS,)),
            dma((SEQS,)),
            dma((phases,)),
            dma((phases,)),
            dma((12,)),
        ],
        compiler_params=pltpu.CompilerParams(
            collective_id=0, has_side_effects=True, vmem_limit_bytes=LIMIT
        ),
        cost_estimate=pl.CostEstimate(
            flops=8 * 10**9, bytes_accessed=10 * 2**20, transcendentals=0
        ),
    )(
        dy.reshape(blocks),
        x.reshape(blocks),
        g,
        aw,
        ao.reshape(blocks),
        wv,
        wo,
        foi,
        foo,
        fvi,
        fvo,
        coef,
        eig,
    )
    return grad_next.reshape(SEQS * LEN, W), scores.T


def solution(mesh):
    nsec = mesh.shape["section"]
    placed = (
        P("section", "tensor"),
        P("section", "tensor"),
        P("section", "tensor"),
        P("section", None, "tensor", None, None),
        P("section", "tensor"),
        P(("section", "tensor"), None),
        P(("section", "tensor"), None),
        P("section", None, "tensor"),
        P("section", None, "tensor"),
        P("section", None, "tensor"),
        P("section", None, "tensor"),
        P("section", None, None, None, None),
        P("section", None, None, None),
    )
    return jax.shard_map(
        functools.partial(per_device, nsec),
        mesh=mesh,
        in_specs=placed,
        out_specs=(P("section", "tensor"), P("section", None)),
        check_vma=False,
    )
```

```python
import functools

import jax
import jax.numpy as jnp
from jax import lax
from jax.experimental import pallas as pl
from jax.experimental.pallas import tpu as pltpu
from jax.sharding import PartitionSpec as P

D = 4096
E = 32
Q = 16
SEQS = 6
LEN = 128
W = 512
HD = 128
T = 8
HALF = LEN // 2
MESH = pl.DeviceIdType.MESH
LIMIT = 64_600_000
LAST = SEQS - 1
SLOTS = SEQS + 1
F32 = jnp.float32
BF16 = jnp.bfloat16
HIGH = lax.Precision.HIGHEST


def contract(left, right):
    return lax.dot_general(left, right, (((1,), (1,)), ((), ())), preferred_element_type=F32)


def lanes_folded(value):
    return value[:, 0:128] + value[:, 128:256] + value[:, 256:384] + value[:, 384:512]


def kernel(
    nsec,
    dy_h,
    x_h,
    g_h,
    aw_h,
    ao_h,
    wv_h,
    wo_h,
    foi_h,
    foo_h,
    fvi_h,
    fvo_h,
    coef_h,
    eig_h,
    gn_h,
    sc_h,
    dyf,
    dvf,
    x_v,
    ao_v,
    aw_v,
    wv_v,
    wo_v,
    fo_v,
    fs_v,
    fp_v,
    fvof,
    g_v,
    coef_v,
    eig_v,
    du_v,
    dx_v,
    p_part,
    p_sib,
    p_snd,
    p_rcv,
    sqt,
    rb,
    mb,
    ev,
    wk,
    sc_v,
    zero_v,
    aw_hi,
    aw_lo,
    rest_v,
    hello,
    lsem,
    dy_ss,
    dy_rs,
    dv_ss,
    dv_rs,
    m_ss,
    m_rs,
    e_ss,
    e_rs,
    xs,
):
    phases = nsec.bit_length() - 1
    s = lax.axis_index("section")
    t = lax.axis_index("tensor")
    core = lax.rem(t, 2)
    chip = t // 2
    right = lax.rem(t + 2, T)
    left = lax.rem(t + 6, T)
    across = lax.rem(t + 4, T)
    sib = t + 1 - 2 * core

    def partner(phase):
        bit = lax.rem(s // 2**phase, 2)
        return s + 2**phase * (1 - 2 * bit)

    def remote(src, dst, ss, rs, **where):
        return pltpu.make_async_remote_copy(
            src_ref=src, dst_ref=dst, send_sem=ss, recv_sem=rs, device_id=where, device_id_type=MESH
        )

    loads = [
        pltpu.make_async_copy(dy_h, dyf.at[t], lsem.at[0]),
        pltpu.make_async_copy(ao_h, ao_v, lsem.at[1]),
        pltpu.make_async_copy(x_h, x_v, lsem.at[2]),
        pltpu.make_async_copy(g_h, g_v, lsem.at[3]),
        pltpu.make_async_copy(foi_h.at[0], fo_v.at[pl.ds(0, E)], lsem.at[4]),
        pltpu.make_async_copy(foo_h.at[0], fs_v.at[pl.ds(E, E)], lsem.at[5]),
        pltpu.make_async_copy(fvi_h.at[0], fp_v.at[pl.ds(2 * E, E)], lsem.at[6]),
        pltpu.make_async_copy(eig_h.at[0], eig_v, lsem.at[7]),
        pltpu.make_async_copy(wo_h, wo_v, lsem.at[8]),
        pltpu.make_async_copy(aw_h.at[0], aw_v, lsem.at[9]),
        pltpu.make_async_copy(wv_h, wv_v, lsem.at[10]),
        pltpu.make_async_copy(coef_h.at[0], coef_v, lsem.at[11]),
        pltpu.make_async_copy(fvo_h.at[0], fvof.at[t, pl.ds(E, E)], lsem.at[12]),
    ]

    fo_v[...] = jnp.zeros_like(fo_v)
    fs_v[...] = jnp.zeros_like(fs_v)
    fp_v[...] = jnp.zeros_like(fp_v)
    fvof[...] = jnp.zeros_like(fvof)

    barrier = pltpu.get_barrier_semaphore()
    for d in range(1, T):
        pl.semaphore_signal(
            barrier, inc=1, device_id={"tensor": lax.rem(t + d, T)}, device_id_type=MESH
        )

    @pl.when(s < nsec - 1)
    def _():
        pl.semaphore_signal(barrier, inc=1, device_id={"section": s + 1}, device_id_type=MESH)

    expected = (T - 1) + (s + nsec - 1) // nsec
    for phase in range(phases):
        upper = lax.rem(s // 2**phase, 2)
        expected += upper

        @pl.when(upper == 0)
        def _():
            pl.semaphore_signal(
                barrier, inc=1, device_id={"section": partner(phase)}, device_id_type=MESH
            )

    for load in loads:
        load.start()
    pl.semaphore_wait(barrier, expected)
    for phase in range(phases):

        @pl.when(lax.rem(s // 2**phase, 2) == 1)
        def _():
            pl.semaphore_signal(
                hello.at[phase], inc=1, device_id={"section": partner(phase)}, device_id_type=MESH
            )

    def ring_routes(first, count):
        half = count // 2
        low, high = pl.ds(first, half), pl.ds(first + half, half)
        whole = pl.ds(first, count)
        return [
            (t, low, right, 0),
            (t, high, left, 0),
            (t, high, right, 1),
            (t, low, left, 1),
            (left, low, right, 2),
            (right, high, left, 2),
            (t, whole, sib, 3),
            (left, whole, sib, 3),
            (right, whole, sib, 3),
            (across, low, sib, 3),
            (across, high, sib, 3),
        ]

    def short_routes(first, count):
        whole = pl.ds(first, count)
        return [
            (t, whole, right, 0),
            (t, whole, left, 0),
            (t, whole, across, 1),
            (t, whole, sib, 3),
            (left, whole, sib, 3),
            (right, whole, sib, 3),
            (across, whole, sib, 3),
        ]

    class Gather:
        def __init__(self, buf, own, ss, rs, slot, b, first, count, routes):
            self.buf, self.own, self.slot = buf, own, slot
            self.ss, self.rs = ss, rs
            self.b, self.rows, self.routes = b, pl.ds(first, count), routes

        def send(self, *kinds):
            for kind in kinds:
                source, rows, target, group = self.routes[kind]
                dst = self.buf.at[source, self.b, rows]
                src = dst
                if self.own is not None and source is t:
                    src = self.own.at[self.b, rows]
                remote(
                    src, dst, self.ss.at[self.slot], self.rs.at[group, self.slot], tensor=target
                ).start()

        def blocks(self, count, group):
            ref = self.buf.at[pl.ds(0, count), self.b, self.rows]
            return remote(
                ref, ref, self.ss.at[self.slot], self.rs.at[group, self.slot], tensor=sib
            )

        def arrived(self, group, count=1):
            self.blocks(count, group).wait_recv()

        def sent(self):
            self.blocks(7, 0).wait_send()

        def spread(self):
            for d in range(1, T):
                ref = self.buf.at[t, self.b, self.rows]
                remote(
                    ref,
                    ref,
                    self.ss.at[self.slot],
                    self.rs.at[3, self.slot],
                    tensor=lax.rem(t + d, T),
                ).start()

    def dy(b):
        return Gather(dyf, dy_h, dy_ss, dy_rs, b, b, 0, LEN, ring_routes(0, LEN))

    def dv(b):
        return Gather(dvf, None, dv_ss, dv_rs, b, b, 0, LEN, ring_routes(0, LEN))

    dy_hi = Gather(dyf, dy_h, dy_ss, dy_rs, LAST, LAST, HALF, HALF, ring_routes(HALF, HALF))
    dy_lo = Gather(dyf, dy_h, dy_ss, dy_rs, SEQS, LAST, 0, HALF, short_routes(0, HALF))
    dv_hi = Gather(dvf, None, dv_ss, dv_rs, LAST, LAST, HALF, HALF, None)
    dv_lo = Gather(dvf, None, dv_ss, dv_rs, SEQS, LAST, 0, HALF, None)
    own_kinds = (0, 1, 2, 3, 6)

    def to_peers(src, dst, ss, rs):
        for d in range(1, T):
            remote(src, dst, ss, rs, tensor=lax.rem(t + d, T)).start()

    def both(ref, ss, rs):
        return remote(ref, ref, ss, rs, tensor=sib)

    def e_copy(phase):
        return remote(
            ev.at[0], ev.at[1 + phase], e_ss.at[phase], e_rs.at[phase], section=partner(phase)
        )

    def ps_copy():
        return remote(p_part.at[1 - core], p_sib, xs.at[0], xs.at[1], tensor=sib)

    def dx_copy(b, rows):
        return remote(
            dx_v.at[b, rows],
            gn_h.at[b, rows],
            xs.at[2],
            xs.at[3],
            section=lax.rem(s + nsec - 1, nsec),
        )

    zero = pltpu.make_async_copy(zero_v, gn_h, lsem.at[13])

    def start_eig(phase):
        @pl.when(lax.rem(s // 2**phase, 2) == 0)
        def _():
            pl.semaphore_wait(hello.at[phase], 1)

        e_copy(phase).start()

    def fold_eig(phase):
        e_copy(phase).wait()
        ev[0] = ev[0] + ev[1 + phase]

    dy(0).send(*own_kinds)
    dy(1).send(*own_kinds)

    loads[7].wait()
    ev[0] = jnp.full((1, 128), jnp.sum(eig_v[0] + eig_v[1]), F32)

    for at in (0, 1, 2, 3, 4, 5, 6):
        loads[at].wait()

    def project(b, carry):
        xf = x_v[b].astype(F32)
        scaled = (xf * g_v[...]).astype(BF16)
        sqt[t, b] = jnp.sum(lanes_folded(xf * xf).T, axis=0, keepdims=True)
        part = contract(ao_v[b], fo_v[...])
        part += contract(dyf[t, b], fs_v[...])
        part += contract(scaled, fp_v[...])
        p_part[lax.rem(b, 2), b // 2] = part
        return carry

    lax.fori_loop(0, SEQS, project, 0)
    to_peers(sqt.at[t], sqt.at[t], xs.at[4], xs.at[5])
    ps_copy().start()

    @pl.when(s == nsec - 1)
    def _():
        zero_v[...] = jnp.zeros_like(zero_v)
        zero.start()

    def value_grad(b):
        dy(b).arrived(3, 4)
        acc = contract(wo_v[:, 0:W], dyf[0, b])
        for k in range(1, T):
            acc += contract(wo_v[:, k * W : (k + 1) * W], dyf[k, b])
        d_att = acc.astype(BF16)
        d_att = jnp.concatenate([d_att[h * HD : (h + 1) * HD] for h in range(4)], axis=1)
        probs = aw_v[b].reshape(4 * LEN, LEN)
        d_val = jnp.dot(d_att, probs, preferred_element_type=F32).T
        dvf[t, b] = d_val.astype(BF16)
        dv(b).send(*own_kinds)

    def half_terms(first, probs):
        rows = pl.ds(first, HALF)
        acc = contract(dyf[0, LAST, rows], wo_v[:, 0:W])
        for k in range(1, T):
            acc += contract(dyf[k, LAST, rows], wo_v[:, k * W : (k + 1) * W])
        d_att = acc.astype(BF16)
        d_att = jnp.concatenate([d_att[:, h * HD : (h + 1) * HD] for h in range(4)], axis=0)
        return jnp.dot(probs, d_att, preferred_element_type=F32)

    def input_grad(slot, b, first, count):
        rows = pl.ds(first, count)
        vals = jnp.concatenate([dvf[k, b, rows] for k in range(T)], axis=1)
        du = contract(vals, wv_v[...])
        du_v[b, rows] = du
        cross = lanes_folded(x_v[b, rows].astype(F32) * g_v[...] * du)
        if count < LEN:
            cross = jnp.concatenate([cross, jnp.zeros((LEN - count, 128), F32)], axis=0)
        mb[slot, t] = jnp.sum(cross.T, axis=0, keepdims=True)
        to_peers(mb.at[slot, t], mb.at[slot, t], m_ss.at[slot], m_rs.at[slot])

    def relay(slot, b, first, count):
        rows = pl.ds(first, count)
        both(mb.at[slot, pl.ds(0, T - 1)], m_ss.at[slot], m_rs.at[slot]).wait_recv()
        total = mb[slot, 0]
        for k in range(1, T):
            total += mb[slot, k]
        mean = jnp.broadcast_to(total * (1.0 / D), (LEN, 128)).T[0:count]
        inv = rb[b, rows]
        cubed = inv * inv * inv * mean
        for k in range(4):
            cols = slice(k * 128, (k + 1) * 128)
            dx = (
                dyf[t, b, rows, cols].astype(F32)
                + inv * g_v[:, cols] * du_v[b, rows, cols]
                - x_v[b, rows, cols].astype(F32) * cubed
            )
            dx_v[b, rows, cols] = dx.astype(BF16)

        @pl.when(s > 0)
        def _():
            dx_copy(b, rows).start()

    def forward_vals(b):
        dv(b).arrived(0)
        dv(b).send(4, 5)
        dv(b).arrived(1)
        dv(b).send(7, 8)

    def finish_vals(b):
        dv(b).arrived(2)
        dv(b).send(9, 10)

    def step(i, carry):
        dy(i).arrived(0)
        dy(i).send(4, 5)

        @pl.when(i >= 1)
        def _():
            dy(i - 1).arrived(2)
            dy(i - 1).send(9, 10)

        dy(i).arrived(1)
        dy(i).send(7, 8)

        @pl.when(i >= 3)
        def _():
            finish_vals(i - 3)

        @pl.when(i >= 2)
        def _():
            forward_vals(i - 2)

        @pl.when(i >= 4)
        def _():
            relay(i - 4, i - 4, 0, LEN)

        @pl.when(i >= 3)
        def _():
            dv(i - 3).arrived(3, 4)
            input_grad(i - 3, i - 3, 0, LEN)

        for phase in range(phases):

            @pl.when(i == phase)
            def _():
                if phase > 0:
                    fold_eig(phase - 1)
                start_eig(phase)

        @pl.when(i == 1)
        def _():
            for at in (8, 9, 10, 11, 12):
                loads[at].wait()
            ps_copy().wait_recv()
            for k in range(3):
                p_snd[k] = p_part[core, k] + p_sib[k]
            both(sqt.at[pl.ds(0, T - 1)], xs.at[4], xs.at[5]).wait_recv()

            def turn(b, carry):
                total = sqt[0, b]
                for k in range(1, T):
                    total += sqt[k, b]
                inv = lax.rsqrt(total * (1.0 / D) + 1e-05)
                rb[b] = jnp.broadcast_to(inv, (LEN, 128)).T
                return carry

            lax.fori_loop(0, SEQS, turn, 0)
            aw_hi[...] = aw_v[LAST, :, HALF:LEN].reshape(4 * HALF, LEN).T
            aw_lo[...] = aw_v[LAST, :, 0:HALF].reshape(4 * HALF, LEN).T

        @pl.when(i >= 1)
        def _():
            value_grad(i - 1)

        @pl.when(i + 2 < LAST)
        def _():
            dy(i + 2).send(*own_kinds)

        @pl.when(i + 2 == LAST)
        def _():
            dy_hi.send(*own_kinds)

        @pl.when(i + 1 == LAST)
        def _():
            dy_lo.send(0, 1, 2, 3)

        return carry

    lax.fori_loop(0, LAST, step, 0)

    dy_hi.arrived(0)
    dy_hi.send(4, 5)
    dy(LAST - 1).arrived(2)
    dy(LAST - 1).send(9, 10)
    dy_hi.arrived(1)
    dy_hi.send(7, 8)
    finish_vals(LAST - 3)
    forward_vals(LAST - 2)
    relay(LAST - 4, LAST - 4, 0, LEN)
    dv(LAST - 3).arrived(3, 4)
    input_grad(LAST - 3, LAST - 3, 0, LEN)
    value_grad(LAST - 1)

    dy_lo.arrived(0, 2)
    dy_lo.send(4, 5)
    dy_hi.arrived(2)
    dy_hi.send(9, 10)
    dy_lo.arrived(1)
    dy_lo.send(6)
    to_peers(fvo_h.at[0], fvof.at[t, pl.ds(E, E)], xs.at[6], xs.at[7])
    for k in range(3):

        @pl.when(chip != k)
        def _():
            slot = lax.rem(chip + 3 - k, 4)
            remote(p_snd.at[k], p_rcv.at[slot], xs.at[8], xs.at[9], tensor=2 * k + core).start()

    dy_hi.arrived(3, 4)
    terms = half_terms(HALF, aw_hi[...])
    rest_v[...] = terms[0:HALF]
    dvf[t, LAST, pl.ds(HALF, HALF)] = terms[HALF:LEN].astype(BF16)
    dv_hi.spread()

    dy_lo.arrived(3, 4)
    terms = half_terms(0, aw_lo[0:HALF])
    dvf[t, LAST, pl.ds(0, HALF)] = (terms + rest_v[...]).astype(BF16)
    dv_lo.spread()

    forward_vals(LAST - 1)
    finish_vals(LAST - 2)
    relay(LAST - 3, LAST - 3, 0, LEN)
    dv(LAST - 2).arrived(3, 4)
    input_grad(LAST - 2, LAST - 2, 0, LEN)
    finish_vals(LAST - 1)
    dv_hi.arrived(3, 7)
    input_grad(LAST, LAST, HALF, HALF)
    dv(LAST - 1).arrived(3, 4)
    input_grad(LAST - 1, LAST - 1, 0, LEN)
    dv_lo.arrived(3, 7)
    input_grad(SEQS, LAST, 0, HALF)
    relay(LAST - 2, LAST - 2, 0, LEN)
    relay(LAST - 1, LAST - 1, 0, LEN)
    relay(LAST, LAST, HALF, HALF)
    relay(SEQS, LAST, 0, HALF)

    fold_eig(phases - 1)
    damp = ev[0] * (0.1 / (nsec * 2 * E * E))
    damp = damp[:, 0:E]
    wk[...] = jnp.zeros_like(wk)
    for m in range(2):
        under = eig_v[m] + damp
        for q in range(Q):
            wk[m * 2 * E : m * 2 * E + E, m * 1024 + q * E : m * 1024 + (q + 1) * E] = (
                coef_v[m, q] / under
            )
    row = lax.broadcasted_iota(jnp.int32, (E, W), 0)
    col = lax.broadcasted_iota(jnp.int32, (E, W), 1)
    wk[E : 2 * E, W : 2 * W] = (lax.rem(col, E) == row).astype(F32)

    both(fvof.at[pl.ds(0, T - 1), pl.ds(E, E)], xs.at[6], xs.at[7]).wait_recv()
    here = sc_h.at[:, pl.ds(pl.multiple_of(t * LEN, LEN), LEN)]
    keep = pltpu.make_async_copy(sc_v, here, lsem.at[14])

    @pl.when(t < SEQS)
    def _():
        both(p_rcv.at[pl.ds(0, 3)], xs.at[8], xs.at[9]).wait_recv()
        proj = p_snd[chip] + p_rcv[0] + p_rcv[1] + p_rcv[2]
        s_val = contract(dvf[0, t], fvof[0])
        for k in range(1, T):
            s_val += contract(dvf[k, t], fvof[k])
        pick = wk[:, W : 2 * W]

        def exact(left, right):
            return jnp.dot(left, right, precision=HIGH, preferred_element_type=F32)

        pairs = exact(proj, wk[:, 0:W]) * exact(proj, pick)
        pairs += exact(proj * rb[t], wk[:, 2 * W : 3 * W]) * exact(s_val, pick)
        row = lax.broadcasted_iota(jnp.int32, (Q, W), 0)
        col = lax.broadcasted_iota(jnp.int32, (Q, W), 1)
        group = (row == col // E).astype(F32)
        sc_v[...] = lax.dot_general(
            group, pairs, (((1,), (1,)), ((), ())), precision=HIGH, preferred_element_type=F32
        )
        keep.start()
        to_peers(sc_v, here, xs.at[10], xs.at[11])

    def drain(b, carry):
        dy(b).sent()
        dv(b).sent()
        return carry

    def drain_sums(slot, carry):
        both(mb.at[slot, pl.ds(0, T - 1)], m_ss.at[slot], m_rs.at[slot]).wait_send()
        return carry

    lax.fori_loop(0, LAST, drain, 0)
    lax.fori_loop(0, SLOTS, drain_sums, 0)
    for gather in (dy_hi, dy_lo, dv_hi, dv_lo):
        gather.sent()
    both(sqt.at[pl.ds(0, T - 1)], xs.at[4], xs.at[5]).wait_send()
    both(fvof.at[pl.ds(0, T - 1), pl.ds(E, E)], xs.at[6], xs.at[7]).wait_send()
    ps_copy().wait_send()

    @pl.when(chip == 3)
    def _():
        both(p_snd.at[pl.ds(0, 3)], xs.at[8], xs.at[9]).wait_send()

    @pl.when(chip < 3)
    def _():
        both(p_snd.at[pl.ds(0, 2)], xs.at[8], xs.at[9]).wait_send()

    @pl.when(s > 0)
    def _():
        both(dx_v, xs.at[2], xs.at[3]).wait_send()

    @pl.when(s < nsec - 1)
    def _():
        both(gn_h, xs.at[2], xs.at[3]).wait_recv()

    @pl.when(s == nsec - 1)
    def _():
        zero.wait()

    @pl.when(t < SEQS)
    def _():
        keep.wait()
        both(wk.at[pl.ds(0, Q), pl.ds(0, 7 * LEN)], xs.at[10], xs.at[11]).wait_send()
        both(sc_h.at[:, pl.ds(0, (SEQS - 1) * LEN)], xs.at[10], xs.at[11]).wait_recv()

    @pl.when(t >= SEQS)
    def _():
        both(sc_h, xs.at[10], xs.at[11]).wait_recv()


def hand_over(gn_h, sc_h, gn_o, sc_o, gn_v, sc_v, in_sem, out_sem):
    pieces = [(gn_h.at[b], gn_v.at[b], gn_o.at[b]) for b in range(SEQS)]
    pieces.append((sc_h, sc_v, sc_o))
    inward = [
        pltpu.make_async_copy(src, mid, in_sem.at[k]) for k, (src, mid, dst) in enumerate(pieces)
    ]
    outward = [
        pltpu.make_async_copy(mid, dst, out_sem.at[k]) for k, (src, mid, dst) in enumerate(pieces)
    ]
    for copy in inward:
        copy.start()
    for first, second in zip(inward, outward):
        first.wait()
        second.start()
    for copy in outward:
        copy.wait()


def per_device(nsec, *arrays):
    (dy, x, g, aw, ao, wv, wo, foi, foo, fvi, fvo, coef, eig) = arrays
    blocks = (SEQS, LEN, W)
    phases = nsec.bit_length() - 1
    dma = pltpu.SemaphoreType.DMA
    vmem = pltpu.VMEM
    grad_next, scores = pl.pallas_call(
        functools.partial(kernel, nsec),
        out_shape=(
            jax.ShapeDtypeStruct(blocks, BF16),
            jax.ShapeDtypeStruct((Q, SEQS * LEN), F32),
        ),
        in_specs=[pl.BlockSpec(memory_space=pltpu.HBM)] * 13,
        out_specs=(pl.BlockSpec(memory_space=pl.ANY), pl.BlockSpec(memory_space=pl.ANY)),
        scratch_shapes=[
            vmem((T, *blocks), BF16),
            vmem((T, SEQS, LEN, HD), BF16),
            vmem(blocks, BF16),
            vmem(blocks, BF16),
            vmem((SEQS, 4, LEN, LEN), BF16),
            vmem((W, 2 * W), BF16),
            vmem((W, D), BF16),
            vmem((128, W), BF16),
            vmem((128, W), BF16),
            vmem((128, W), BF16),
            vmem((T, 128, HD), BF16),
            vmem((1, W), F32),
            vmem((2, Q, E, E), F32),
            vmem((2, E, E), F32),
            vmem(blocks, F32),
            vmem(blocks, BF16),
            vmem((2, 3, LEN, 128), F32),
            vmem((3, LEN, 128), F32),
            vmem((3, LEN, 128), F32),
            vmem((3, LEN, 128), F32),
            vmem((T, SEQS, 1, 128), F32),
            vmem((SEQS, LEN, 128), F32),
            vmem((SLOTS, T, 1, 128), F32),
            vmem((1 + phases, 1, 128), F32),
            vmem((128, 3 * W), F32),
            vmem((Q, LEN), F32),
            vmem(blocks, BF16),
            vmem((LEN, 4 * HALF), BF16),
            vmem((LEN, 4 * HALF), BF16),
            vmem((HALF, HD), F32),
            pltpu.SemaphoreType.REGULAR((phases,)),
            dma((15,)),
            dma((SLOTS,)),
            dma((4, SLOTS)),
            dma((SLOTS,)),
            dma((4, SLOTS)),
            dma((SLOTS,)),
            dma((SLOTS,)),
            dma((phases,)),
            dma((phases,)),
            dma((12,)),
        ],
        compiler_params=pltpu.CompilerParams(
            collective_id=0, has_side_effects=True, vmem_limit_bytes=LIMIT
        ),
        cost_estimate=pl.CostEstimate(
            flops=8 * 10**9, bytes_accessed=10 * 2**20, transcendentals=0
        ),
    )(
        dy.reshape(blocks),
        x.reshape(blocks),
        g,
        aw,
        ao.reshape(blocks),
        wv,
        wo,
        foi,
        foo,
        fvi,
        fvo,
        coef,
        eig,
    )
    grad_next, scores = pl.pallas_call(
        hand_over,
        out_shape=(
            jax.ShapeDtypeStruct(blocks, BF16),
            jax.ShapeDtypeStruct((Q, SEQS * LEN), F32),
        ),
        in_specs=[pl.BlockSpec(memory_space=pl.ANY)] * 2,
        out_specs=(pl.BlockSpec(memory_space=pl.ANY), pl.BlockSpec(memory_space=pl.ANY)),
        scratch_shapes=[
            vmem(blocks, BF16),
            vmem((Q, SEQS * LEN), F32),
            dma((SEQS + 1,)),
            dma((SEQS + 1,)),
        ],
        compiler_params=pltpu.CompilerParams(vmem_limit_bytes=LIMIT),
    )(grad_next, scores)
    return grad_next.reshape(SEQS * LEN, W), scores.T


def solution(mesh):
    nsec = mesh.shape["section"]
    placed = (
        P("section", "tensor"),
        P("section", "tensor"),
        P("section", "tensor"),
        P("section", None, "tensor", None, None),
        P("section", "tensor"),
        P(("section", "tensor"), None),
        P(("section", "tensor"), None),
        P("section", None, "tensor"),
        P("section", None, "tensor"),
        P("section", None, "tensor"),
        P("section", None, "tensor"),
        P("section", None, None, None, None),
        P("section", None, None, None),
    )
    return jax.shard_map(
        functools.partial(per_device, nsec),
        mesh=mesh,
        in_specs=placed,
        out_specs=(P("section", "tensor"), P("section", None)),
        check_vma=False,
    )
```

```python
import functools

import jax
import jax.numpy as jnp
from jax import lax
from jax.experimental import pallas as pl
from jax.experimental.pallas import tpu as pltpu
from jax.sharding import PartitionSpec as P

D = 4096
E = 32
Q = 16
SEQS = 6
LEN = 128
W = 512
HD = 128
T = 8
HALF = LEN // 2
MESH = pl.DeviceIdType.MESH
LIMIT = 64_600_000
LAST = SEQS - 1
SLOTS = SEQS + 1
F32 = jnp.float32
BF16 = jnp.bfloat16
HIGH = lax.Precision.HIGHEST


def contract(left, right):
    return lax.dot_general(left, right, (((1,), (1,)), ((), ())), preferred_element_type=F32)


def lanes_folded(value):
    return value[:, 0:128] + value[:, 128:256] + value[:, 256:384] + value[:, 384:512]


def kernel(
    nsec,
    dy_h,
    x_h,
    g_h,
    aw_h,
    ao_h,
    wv_h,
    wo_h,
    foi_h,
    foo_h,
    fvi_h,
    fvo_h,
    coef_h,
    eig_h,
    gn_h,
    sc_h,
    dyf,
    dvf,
    x_v,
    ao_v,
    aw_v,
    wv_v,
    wo_v,
    fo_v,
    fs_v,
    fp_v,
    fvof,
    g_v,
    coef_v,
    eig_v,
    du_v,
    dx_v,
    p_part,
    p_sib,
    p_snd,
    p_rcv,
    sqt,
    rb,
    mb,
    ev,
    wk,
    sc_v,
    zero_v,
    aw_hi,
    aw_lo,
    rest_v,
    hello,
    lsem,
    dy_ss,
    dy_rs,
    dv_ss,
    dv_rs,
    m_ss,
    m_rs,
    e_ss,
    e_rs,
    xs,
):
    phases = nsec.bit_length() - 1
    s = lax.axis_index("section")
    t = lax.axis_index("tensor")
    core = lax.rem(t, 2)
    chip = t // 2
    right = lax.rem(t + 2, T)
    left = lax.rem(t + 6, T)
    across = lax.rem(t + 4, T)
    sib = t + 1 - 2 * core

    def partner(phase):
        bit = lax.rem(s // 2**phase, 2)
        return s + 2**phase * (1 - 2 * bit)

    def remote(src, dst, ss, rs, **where):
        return pltpu.make_async_remote_copy(
            src_ref=src, dst_ref=dst, send_sem=ss, recv_sem=rs, device_id=where, device_id_type=MESH
        )

    loads = [
        pltpu.make_async_copy(dy_h, dyf.at[t], lsem.at[0]),
        pltpu.make_async_copy(ao_h, ao_v, lsem.at[1]),
        pltpu.make_async_copy(x_h, x_v, lsem.at[2]),
        pltpu.make_async_copy(g_h, g_v, lsem.at[3]),
        pltpu.make_async_copy(foi_h.at[0], fo_v.at[pl.ds(0, E)], lsem.at[4]),
        pltpu.make_async_copy(foo_h.at[0], fs_v.at[pl.ds(E, E)], lsem.at[5]),
        pltpu.make_async_copy(fvi_h.at[0], fp_v.at[pl.ds(2 * E, E)], lsem.at[6]),
        pltpu.make_async_copy(eig_h.at[0], eig_v, lsem.at[7]),
        pltpu.make_async_copy(wo_h, wo_v, lsem.at[8]),
        pltpu.make_async_copy(aw_h.at[0], aw_v, lsem.at[9]),
        pltpu.make_async_copy(wv_h, wv_v, lsem.at[10]),
        pltpu.make_async_copy(coef_h.at[0], coef_v, lsem.at[11]),
        pltpu.make_async_copy(fvo_h.at[0], fvof.at[t, pl.ds(E, E)], lsem.at[12]),
    ]

    fo_v[...] = jnp.zeros_like(fo_v)
    fs_v[...] = jnp.zeros_like(fs_v)
    fp_v[...] = jnp.zeros_like(fp_v)
    fvof[...] = jnp.zeros_like(fvof)

    barrier = pltpu.get_barrier_semaphore()
    for d in range(1, T):
        pl.semaphore_signal(
            barrier, inc=1, device_id={"tensor": lax.rem(t + d, T)}, device_id_type=MESH
        )

    @pl.when(s < nsec - 1)
    def _():
        pl.semaphore_signal(barrier, inc=1, device_id={"section": s + 1}, device_id_type=MESH)

    expected = (T - 1) + (s + nsec - 1) // nsec
    for phase in range(phases):
        upper = lax.rem(s // 2**phase, 2)
        expected += upper

        @pl.when(upper == 0)
        def _():
            pl.semaphore_signal(
                barrier, inc=1, device_id={"section": partner(phase)}, device_id_type=MESH
            )

    for load in loads:
        load.start()
    pl.semaphore_wait(barrier, expected)
    for phase in range(phases):

        @pl.when(lax.rem(s // 2**phase, 2) == 1)
        def _():
            pl.semaphore_signal(
                hello.at[phase], inc=1, device_id={"section": partner(phase)}, device_id_type=MESH
            )

    def ring_routes(first, count):
        half = count // 2
        low, high = pl.ds(first, half), pl.ds(first + half, half)
        whole = pl.ds(first, count)
        return [
            (t, low, right, 0),
            (t, high, left, 0),
            (t, high, right, 1),
            (t, low, left, 1),
            (left, low, right, 2),
            (right, high, left, 2),
            (t, whole, sib, 3),
            (left, whole, sib, 3),
            (right, whole, sib, 3),
            (across, low, sib, 3),
            (across, high, sib, 3),
        ]

    def short_routes(first, count):
        whole = pl.ds(first, count)
        return [
            (t, whole, right, 0),
            (t, whole, left, 0),
            (t, whole, across, 1),
            (t, whole, sib, 3),
            (left, whole, sib, 3),
            (right, whole, sib, 3),
            (across, whole, sib, 3),
        ]

    class Gather:
        def __init__(self, buf, own, ss, rs, slot, b, first, count, routes):
            self.buf, self.own, self.slot = buf, own, slot
            self.ss, self.rs = ss, rs
            self.b, self.rows, self.routes = b, pl.ds(first, count), routes

        def send(self, *kinds):
            for kind in kinds:
                source, rows, target, group = self.routes[kind]
                dst = self.buf.at[source, self.b, rows]
                src = dst
                if self.own is not None and source is t:
                    src = self.own.at[self.b, rows]
                remote(
                    src, dst, self.ss.at[self.slot], self.rs.at[group, self.slot], tensor=target
                ).start()

        def blocks(self, count, group):
            ref = self.buf.at[pl.ds(0, count), self.b, self.rows]
            return remote(
                ref, ref, self.ss.at[self.slot], self.rs.at[group, self.slot], tensor=sib
            )

        def arrived(self, group, count=1):
            self.blocks(count, group).wait_recv()

        def sent(self):
            self.blocks(7, 0).wait_send()

        def spread(self):
            for d in range(1, T):
                ref = self.buf.at[t, self.b, self.rows]
                remote(
                    ref,
                    ref,
                    self.ss.at[self.slot],
                    self.rs.at[3, self.slot],
                    tensor=lax.rem(t + d, T),
                ).start()

    def dy(b):
        return Gather(dyf, dy_h, dy_ss, dy_rs, b, b, 0, LEN, ring_routes(0, LEN))

    def dv(b):
        return Gather(dvf, None, dv_ss, dv_rs, b, b, 0, LEN, short_routes(0, LEN))

    dy_hi = Gather(dyf, dy_h, dy_ss, dy_rs, LAST, LAST, HALF, HALF, ring_routes(HALF, HALF))
    dy_lo = Gather(dyf, dy_h, dy_ss, dy_rs, SEQS, LAST, 0, HALF, short_routes(0, HALF))
    dv_hi = Gather(dvf, None, dv_ss, dv_rs, LAST, LAST, HALF, HALF, short_routes(HALF, HALF))
    dv_lo = Gather(dvf, None, dv_ss, dv_rs, SEQS, LAST, 0, HALF, short_routes(0, HALF))
    own_kinds = (0, 1, 2, 3, 6)
    short_kinds = (2, 0, 1, 3)

    def to_peers(src, dst, ss, rs):
        for d in range(1, T):
            remote(src, dst, ss, rs, tensor=lax.rem(t + d, T)).start()

    def both(ref, ss, rs):
        return remote(ref, ref, ss, rs, tensor=sib)

    def e_copy(phase):
        return remote(
            ev.at[0], ev.at[1 + phase], e_ss.at[phase], e_rs.at[phase], section=partner(phase)
        )

    def ps_copy():
        return remote(p_part.at[1 - core], p_sib, xs.at[0], xs.at[1], tensor=sib)

    def dx_copy(b, rows):
        return remote(
            dx_v.at[b, rows],
            gn_h.at[b, rows],
            xs.at[2],
            xs.at[3],
            section=lax.rem(s + nsec - 1, nsec),
        )

    zero = pltpu.make_async_copy(zero_v, gn_h, lsem.at[13])

    def start_eig(phase):
        @pl.when(lax.rem(s // 2**phase, 2) == 0)
        def _():
            pl.semaphore_wait(hello.at[phase], 1)

        e_copy(phase).start()

    def fold_eig(phase):
        e_copy(phase).wait()
        ev[0] = ev[0] + ev[1 + phase]

    dy(0).send(*own_kinds)
    dy(1).send(*own_kinds)

    loads[7].wait()
    ev[0] = jnp.full((1, 128), jnp.sum(eig_v[0] + eig_v[1]), F32)

    for at in (0, 1, 2, 3, 4, 5, 6):
        loads[at].wait()

    def project(b, carry):
        xf = x_v[b].astype(F32)
        scaled = (xf * g_v[...]).astype(BF16)
        sqt[t, b] = jnp.sum(lanes_folded(xf * xf).T, axis=0, keepdims=True)
        part = contract(ao_v[b], fo_v[...])
        part += contract(dyf[t, b], fs_v[...])
        part += contract(scaled, fp_v[...])
        p_part[lax.rem(b, 2), b // 2] = part
        return carry

    lax.fori_loop(0, SEQS, project, 0)
    to_peers(sqt.at[t], sqt.at[t], xs.at[4], xs.at[5])
    ps_copy().start()

    @pl.when(s == nsec - 1)
    def _():
        zero_v[...] = jnp.zeros_like(zero_v)
        zero.start()

    def value_grad(b):
        dy(b).arrived(3, 4)
        acc = contract(wo_v[:, 0:W], dyf[0, b])
        for k in range(1, T):
            acc += contract(wo_v[:, k * W : (k + 1) * W], dyf[k, b])
        d_att = acc.astype(BF16)
        d_att = jnp.concatenate([d_att[h * HD : (h + 1) * HD] for h in range(4)], axis=1)
        probs = aw_v[b].reshape(4 * LEN, LEN)
        d_val = jnp.dot(d_att, probs, preferred_element_type=F32).T
        dvf[t, b] = d_val.astype(BF16)
        dv(b).send(*short_kinds)

    def half_terms(first, probs):
        rows = pl.ds(first, HALF)
        acc = contract(dyf[0, LAST, rows], wo_v[:, 0:W])
        for k in range(1, T):
            acc += contract(dyf[k, LAST, rows], wo_v[:, k * W : (k + 1) * W])
        d_att = acc.astype(BF16)
        d_att = jnp.concatenate([d_att[:, h * HD : (h + 1) * HD] for h in range(4)], axis=0)
        return jnp.dot(probs, d_att, preferred_element_type=F32)

    def input_grad(slot, b, first, count):
        rows = pl.ds(first, count)
        vals = jnp.concatenate([dvf[k, b, rows] for k in range(T)], axis=1)
        du = contract(vals, wv_v[...])
        du_v[b, rows] = du
        cross = lanes_folded(x_v[b, rows].astype(F32) * g_v[...] * du)
        if count < LEN:
            cross = jnp.concatenate([cross, jnp.zeros((LEN - count, 128), F32)], axis=0)
        mb[slot, t] = jnp.sum(cross.T, axis=0, keepdims=True)
        to_peers(mb.at[slot, t], mb.at[slot, t], m_ss.at[slot], m_rs.at[slot])

    def relay(slot, b, first, count):
        rows = pl.ds(first, count)
        both(mb.at[slot, pl.ds(0, T - 1)], m_ss.at[slot], m_rs.at[slot]).wait_recv()
        total = mb[slot, 0]
        for k in range(1, T):
            total += mb[slot, k]
        mean = jnp.broadcast_to(total * (1.0 / D), (LEN, 128)).T[0:count]
        inv = rb[b, rows]
        cubed = inv * inv * inv * mean
        for k in range(4):
            cols = slice(k * 128, (k + 1) * 128)
            dx = (
                dyf[t, b, rows, cols].astype(F32)
                + inv * g_v[:, cols] * du_v[b, rows, cols]
                - x_v[b, rows, cols].astype(F32) * cubed
            )
            dx_v[b, rows, cols] = dx.astype(BF16)

        @pl.when(s > 0)
        def _():
            dx_copy(b, rows).start()

    def share_vals(gather):
        gather.arrived(0, 2)
        gather.send(4, 5)
        gather.arrived(1)
        gather.send(6)

    def step(i, carry):
        dy(i).arrived(0)
        dy(i).send(4, 5)

        @pl.when(i >= 1)
        def _():
            dy(i - 1).arrived(2)
            dy(i - 1).send(9, 10)

        dy(i).arrived(1)
        dy(i).send(7, 8)

        @pl.when(i >= 3)
        def _():
            dv(i - 3).arrived(3, 4)
            input_grad(i - 3, i - 3, 0, LEN)

        for phase in range(phases):

            @pl.when(i == phase)
            def _():
                if phase > 0:
                    fold_eig(phase - 1)
                start_eig(phase)

        @pl.when(i == 1)
        def _():
            for at in (8, 9, 10, 11, 12):
                loads[at].wait()
            ps_copy().wait_recv()
            for k in range(3):
                p_snd[k] = p_part[core, k] + p_sib[k]

        @pl.when(i >= 1)
        def _():
            value_grad(i - 1)

        @pl.when(i + 2 < LAST)
        def _():
            dy(i + 2).send(*own_kinds)

        @pl.when(i + 2 == LAST)
        def _():
            dy_hi.send(*own_kinds)

        @pl.when(i + 1 == LAST)
        def _():
            dy_lo.send(0, 1, 2, 3)

        @pl.when(i == 2)
        def _():
            both(sqt.at[pl.ds(0, T - 1)], xs.at[4], xs.at[5]).wait_recv()

            def turn(b, carry):
                total = sqt[0, b]
                for k in range(1, T):
                    total += sqt[k, b]
                inv = lax.rsqrt(total * (1.0 / D) + 1e-05)
                rb[b] = jnp.broadcast_to(inv, (LEN, 128)).T
                return carry

            lax.fori_loop(0, SEQS, turn, 0)
            aw_hi[...] = aw_v[LAST, :, HALF:LEN].reshape(4 * HALF, LEN).T
            aw_lo[...] = aw_v[LAST, :, 0:HALF].reshape(4 * HALF, LEN).T

        @pl.when(i >= 2)
        def _():
            share_vals(dv(i - 2))

        @pl.when(i >= 3)
        def _():
            relay(i - 3, i - 3, 0, LEN)

        return carry

    lax.fori_loop(0, LAST, step, 0)

    dy_hi.arrived(0)
    dy_hi.send(4, 5)
    dy(LAST - 1).arrived(2)
    dy(LAST - 1).send(9, 10)
    dy_hi.arrived(1)
    dy_hi.send(7, 8)
    dv(LAST - 3).arrived(3, 4)
    input_grad(LAST - 3, LAST - 3, 0, LEN)
    value_grad(LAST - 1)

    dy_lo.arrived(0, 2)
    dy_lo.send(4, 5)
    dy_hi.arrived(2)
    dy_hi.send(9, 10)
    share_vals(dv(LAST - 2))
    dy_lo.arrived(1)
    dy_lo.send(6)
    relay(LAST - 3, LAST - 3, 0, LEN)
    to_peers(fvo_h.at[0], fvof.at[t, pl.ds(E, E)], xs.at[6], xs.at[7])
    for k in range(3):

        @pl.when(chip != k)
        def _():
            slot = lax.rem(chip + 3 - k, 4)
            remote(
                p_snd.at[k], p_rcv.at[slot], xs.at[8], xs.at[9], tensor=2 * k + core
            ).start()

    dy_hi.arrived(3, 4)
    terms = half_terms(HALF, aw_hi[...])
    rest_v[...] = terms[0:HALF]
    dvf[t, LAST, pl.ds(HALF, HALF)] = terms[HALF:LEN].astype(BF16)
    dv_hi.send(*short_kinds)
    dv(LAST - 2).arrived(3, 4)
    input_grad(LAST - 2, LAST - 2, 0, LEN)

    dy_lo.arrived(3, 4)
    terms = half_terms(0, aw_lo[0:HALF])
    dvf[t, LAST, pl.ds(0, HALF)] = (terms + rest_v[...]).astype(BF16)
    dv_lo.send(*short_kinds)

    share_vals(dv(LAST - 1))
    share_vals(dv_hi)
    relay(LAST - 2, LAST - 2, 0, LEN)
    dv(LAST - 1).arrived(3, 4)
    input_grad(LAST - 1, LAST - 1, 0, LEN)
    share_vals(dv_lo)
    dv_hi.arrived(3, 4)
    input_grad(LAST, LAST, HALF, HALF)
    dv_lo.arrived(3, 4)
    input_grad(SEQS, LAST, 0, HALF)
    relay(LAST - 1, LAST - 1, 0, LEN)
    relay(LAST, LAST, HALF, HALF)
    relay(SEQS, LAST, 0, HALF)

    fold_eig(phases - 1)
    damp = ev[0] * (0.1 / (nsec * 2 * E * E))
    damp = damp[:, 0:E]
    wk[...] = jnp.zeros_like(wk)
    for m in range(2):
        under = eig_v[m] + damp
        for q in range(Q):
            wk[m * 2 * E : m * 2 * E + E, m * 1024 + q * E : m * 1024 + (q + 1) * E] = (
                coef_v[m, q] / under
            )
    row = lax.broadcasted_iota(jnp.int32, (E, W), 0)
    col = lax.broadcasted_iota(jnp.int32, (E, W), 1)
    wk[E : 2 * E, W : 2 * W] = (lax.rem(col, E) == row).astype(F32)

    both(fvof.at[pl.ds(0, T - 1), pl.ds(E, E)], xs.at[6], xs.at[7]).wait_recv()
    here = sc_h.at[:, pl.ds(pl.multiple_of(t * LEN, LEN), LEN)]
    keep = pltpu.make_async_copy(sc_v, here, lsem.at[14])

    @pl.when(t < SEQS)
    def _():
        both(p_rcv.at[pl.ds(0, 3)], xs.at[8], xs.at[9]).wait_recv()
        proj = p_snd[chip] + p_rcv[0] + p_rcv[1] + p_rcv[2]
        s_val = contract(dvf[0, t], fvof[0])
        for k in range(1, T):
            s_val += contract(dvf[k, t], fvof[k])
        pick = wk[:, W : 2 * W]

        def exact(left, right):
            return jnp.dot(left, right, precision=HIGH, preferred_element_type=F32)

        pairs = exact(proj, wk[:, 0:W]) * exact(proj, pick)
        pairs += exact(proj * rb[t], wk[:, 2 * W : 3 * W]) * exact(s_val, pick)
        row = lax.broadcasted_iota(jnp.int32, (Q, W), 0)
        col = lax.broadcasted_iota(jnp.int32, (Q, W), 1)
        group = (row == col // E).astype(F32)
        sc_v[...] = lax.dot_general(
            group, pairs, (((1,), (1,)), ((), ())), precision=HIGH, preferred_element_type=F32
        )
        keep.start()
        to_peers(sc_v, here, xs.at[10], xs.at[11])

    def drain(b, carry):
        dy(b).sent()
        dv(b).sent()
        return carry

    def drain_sums(slot, carry):
        both(mb.at[slot, pl.ds(0, T - 1)], m_ss.at[slot], m_rs.at[slot]).wait_send()
        return carry

    lax.fori_loop(0, LAST, drain, 0)
    lax.fori_loop(0, SLOTS, drain_sums, 0)
    for gather in (dy_hi, dy_lo, dv_hi, dv_lo):
        gather.sent()
    both(sqt.at[pl.ds(0, T - 1)], xs.at[4], xs.at[5]).wait_send()
    both(fvof.at[pl.ds(0, T - 1), pl.ds(E, E)], xs.at[6], xs.at[7]).wait_send()
    ps_copy().wait_send()

    @pl.when(chip == 3)
    def _():
        both(p_snd.at[pl.ds(0, 3)], xs.at[8], xs.at[9]).wait_send()

    @pl.when(chip < 3)
    def _():
        both(p_snd.at[pl.ds(0, 2)], xs.at[8], xs.at[9]).wait_send()

    @pl.when(s > 0)
    def _():
        both(dx_v, xs.at[2], xs.at[3]).wait_send()

    @pl.when(s < nsec - 1)
    def _():
        both(gn_h, xs.at[2], xs.at[3]).wait_recv()

    @pl.when(s == nsec - 1)
    def _():
        zero.wait()

    @pl.when(t < SEQS)
    def _():
        keep.wait()
        both(wk.at[pl.ds(0, Q), pl.ds(0, 7 * LEN)], xs.at[10], xs.at[11]).wait_send()
        both(sc_h.at[:, pl.ds(0, (SEQS - 1) * LEN)], xs.at[10], xs.at[11]).wait_recv()

    @pl.when(t >= SEQS)
    def _():
        both(sc_h, xs.at[10], xs.at[11]).wait_recv()


def hand_over(gn_h, sc_h, gn_o, sc_o, gn_v, sc_v, in_sem, out_sem):
    pieces = [(gn_h.at[b], gn_v.at[b], gn_o.at[b]) for b in range(SEQS)]
    pieces.append((sc_h, sc_v, sc_o))
    inward = [
        pltpu.make_async_copy(src, mid, in_sem.at[k]) for k, (src, mid, dst) in enumerate(pieces)
    ]
    outward = [
        pltpu.make_async_copy(mid, dst, out_sem.at[k]) for k, (src, mid, dst) in enumerate(pieces)
    ]
    for copy in inward:
        copy.start()
    for first, second in zip(inward, outward):
        first.wait()
        second.start()
    for copy in outward:
        copy.wait()


def per_device(nsec, *arrays):
    (dy, x, g, aw, ao, wv, wo, foi, foo, fvi, fvo, coef, eig) = arrays
    blocks = (SEQS, LEN, W)
    phases = nsec.bit_length() - 1
    dma = pltpu.SemaphoreType.DMA
    vmem = pltpu.VMEM
    grad_next, scores = pl.pallas_call(
        functools.partial(kernel, nsec),
        out_shape=(
            jax.ShapeDtypeStruct(blocks, BF16),
            jax.ShapeDtypeStruct((Q, SEQS * LEN), F32),
        ),
        in_specs=[pl.BlockSpec(memory_space=pltpu.HBM)] * 13,
        out_specs=(pl.BlockSpec(memory_space=pl.ANY), pl.BlockSpec(memory_space=pl.ANY)),
        scratch_shapes=[
            vmem((T, *blocks), BF16),
            vmem((T, SEQS, LEN, HD), BF16),
            vmem(blocks, BF16),
            vmem(blocks, BF16),
            vmem((SEQS, 4, LEN, LEN), BF16),
            vmem((W, 2 * W), BF16),
            vmem((W, D), BF16),
            vmem((128, W), BF16),
            vmem((128, W), BF16),
            vmem((128, W), BF16),
            vmem((T, 128, HD), BF16),
            vmem((1, W), F32),
            vmem((2, Q, E, E), F32),
            vmem((2, E, E), F32),
            vmem(blocks, F32),
            vmem(blocks, BF16),
            vmem((2, 3, LEN, 128), F32),
            vmem((3, LEN, 128), F32),
            vmem((3, LEN, 128), F32),
            vmem((3, LEN, 128), F32),
            vmem((T, SEQS, 1, 128), F32),
            vmem((SEQS, LEN, 128), F32),
            vmem((SLOTS, T, 1, 128), F32),
            vmem((1 + phases, 1, 128), F32),
            vmem((128, 3 * W), F32),
            vmem((Q, LEN), F32),
            vmem(blocks, BF16),
            vmem((LEN, 4 * HALF), BF16),
            vmem((LEN, 4 * HALF), BF16),
            vmem((HALF, HD), F32),
            pltpu.SemaphoreType.REGULAR((phases,)),
            dma((15,)),
            dma((SLOTS,)),
            dma((4, SLOTS)),
            dma((SLOTS,)),
            dma((4, SLOTS)),
            dma((SLOTS,)),
            dma((SLOTS,)),
            dma((phases,)),
            dma((phases,)),
            dma((12,)),
        ],
        compiler_params=pltpu.CompilerParams(
            collective_id=0, has_side_effects=True, vmem_limit_bytes=LIMIT
        ),
        cost_estimate=pl.CostEstimate(
            flops=8 * 10**9, bytes_accessed=10 * 2**20, transcendentals=0
        ),
    )(
        dy.reshape(blocks),
        x.reshape(blocks),
        g,
        aw,
        ao.reshape(blocks),
        wv,
        wo,
        foi,
        foo,
        fvi,
        fvo,
        coef,
        eig,
    )
    grad_next, scores = pl.pallas_call(
        hand_over,
        out_shape=(
            jax.ShapeDtypeStruct(blocks, BF16),
            jax.ShapeDtypeStruct((Q, SEQS * LEN), F32),
        ),
        in_specs=[pl.BlockSpec(memory_space=pl.ANY)] * 2,
        out_specs=(pl.BlockSpec(memory_space=pl.ANY), pl.BlockSpec(memory_space=pl.ANY)),
        scratch_shapes=[
            vmem(blocks, BF16),
            vmem((Q, SEQS * LEN), F32),
            dma((SEQS + 1,)),
            dma((SEQS + 1,)),
        ],
        compiler_params=pltpu.CompilerParams(vmem_limit_bytes=LIMIT),
    )(grad_next, scores)
    return grad_next.reshape(SEQS * LEN, W), scores.T


def solution(mesh):
    nsec = mesh.shape["section"]
    placed = (
        P("section", "tensor"),
        P("section", "tensor"),
        P("section", "tensor"),
        P("section", None, "tensor", None, None),
        P("section", "tensor"),
        P(("section", "tensor"), None),
        P(("section", "tensor"), None),
        P("section", None, "tensor"),
        P("section", None, "tensor"),
        P("section", None, "tensor"),
        P("section", None, "tensor"),
        P("section", None, None, None, None),
        P("section", None, None, None),
    )
    return jax.shard_map(
        functools.partial(per_device, nsec),
        mesh=mesh,
        in_specs=placed,
        out_specs=(P("section", "tensor"), P("section", None)),
        check_vma=False,
    )
```

```python
import functools

import jax
import jax.numpy as jnp
from jax import lax
from jax.experimental import pallas as pl
from jax.experimental.pallas import tpu as pltpu
from jax.sharding import PartitionSpec as P

D = 4096
E = 32
Q = 16
SEQS = 6
LEN = 128
W = 512
HD = 128
T = 8
LOW = 32
REST = LEN - LOW
MESH = pl.DeviceIdType.MESH
LIMIT = 64_600_000
LAST = SEQS - 1
SLOTS = SEQS + 1
F32 = jnp.float32
BF16 = jnp.bfloat16
HIGH = lax.Precision.HIGHEST


def contract(left, right):
    return lax.dot_general(left, right, (((1,), (1,)), ((), ())), preferred_element_type=F32)


def lanes_folded(value):
    return value[:, 0:128] + value[:, 128:256] + value[:, 256:384] + value[:, 384:512]


def kernel(
    nsec,
    dy_h,
    x_h,
    g_h,
    aw_h,
    ao_h,
    wv_h,
    wo_h,
    foi_h,
    foo_h,
    fvi_h,
    fvo_h,
    coef_h,
    eig_h,
    gn_h,
    sc_h,
    dyf,
    dvf,
    x_v,
    ao_v,
    aw_v,
    wv_v,
    wo_v,
    fo_v,
    fs_v,
    fp_v,
    fvof,
    g_v,
    coef_v,
    eig_v,
    du_v,
    dx_v,
    p_part,
    p_sib,
    p_snd,
    p_rcv,
    sqt,
    rb,
    mb,
    ev,
    wk,
    sc_v,
    zero_v,
    aw_hi,
    aw_lo,
    rest_v,
    hello,
    lsem,
    dy_ss,
    dy_rs,
    dv_ss,
    dv_rs,
    m_ss,
    m_rs,
    e_ss,
    e_rs,
    fv_ss,
    fv_rs,
    xs,
):
    phases = nsec.bit_length() - 1
    s = lax.axis_index("section")
    t = lax.axis_index("tensor")
    core = lax.rem(t, 2)
    chip = t // 2
    right = lax.rem(t + 2, T)
    left = lax.rem(t + 6, T)
    across = lax.rem(t + 4, T)
    sib = t + 1 - 2 * core

    def partner(phase):
        bit = lax.rem(s // 2**phase, 2)
        return s + 2**phase * (1 - 2 * bit)

    def remote(src, dst, ss, rs, **where):
        return pltpu.make_async_remote_copy(
            src_ref=src, dst_ref=dst, send_sem=ss, recv_sem=rs, device_id=where, device_id_type=MESH
        )

    loads = [
        pltpu.make_async_copy(dy_h, dyf.at[t], lsem.at[0]),
        pltpu.make_async_copy(ao_h, ao_v, lsem.at[1]),
        pltpu.make_async_copy(x_h, x_v, lsem.at[2]),
        pltpu.make_async_copy(g_h, g_v, lsem.at[3]),
        pltpu.make_async_copy(foi_h.at[0], fo_v.at[pl.ds(0, E)], lsem.at[4]),
        pltpu.make_async_copy(foo_h.at[0], fs_v.at[pl.ds(E, E)], lsem.at[5]),
        pltpu.make_async_copy(fvi_h.at[0], fp_v.at[pl.ds(2 * E, E)], lsem.at[6]),
        pltpu.make_async_copy(eig_h.at[0], eig_v, lsem.at[7]),
        pltpu.make_async_copy(wo_h, wo_v, lsem.at[8]),
        pltpu.make_async_copy(aw_h.at[0], aw_v, lsem.at[9]),
        pltpu.make_async_copy(wv_h, wv_v, lsem.at[10]),
        pltpu.make_async_copy(coef_h.at[0], coef_v, lsem.at[11]),
        pltpu.make_async_copy(fvo_h.at[0], fvof.at[t, 0, pl.ds(E, E)], lsem.at[12]),
    ]

    fo_v[...] = jnp.zeros_like(fo_v)
    fs_v[...] = jnp.zeros_like(fs_v)
    fp_v[...] = jnp.zeros_like(fp_v)
    fvof[...] = jnp.zeros_like(fvof)

    barrier = pltpu.get_barrier_semaphore()
    for d in range(1, T):
        pl.semaphore_signal(
            barrier, inc=1, device_id={"tensor": lax.rem(t + d, T)}, device_id_type=MESH
        )

    @pl.when(s < nsec - 1)
    def _():
        pl.semaphore_signal(barrier, inc=1, device_id={"section": s + 1}, device_id_type=MESH)

    expected = (T - 1) + (s + nsec - 1) // nsec
    for phase in range(phases):
        upper = lax.rem(s // 2**phase, 2)
        expected += upper

        @pl.when(upper == 0)
        def _():
            pl.semaphore_signal(
                barrier, inc=1, device_id={"section": partner(phase)}, device_id_type=MESH
            )

    for load in loads:
        load.start()
    pl.semaphore_wait(barrier, expected)
    for phase in range(phases):

        @pl.when(lax.rem(s // 2**phase, 2) == 1)
        def _():
            pl.semaphore_signal(
                hello.at[phase], inc=1, device_id={"section": partner(phase)}, device_id_type=MESH
            )

    def ring_routes(first, count):
        half = count // 2
        low, high = pl.ds(first, half), pl.ds(first + half, half)
        whole = pl.ds(first, count)
        return [
            (t, low, right, 0),
            (t, high, left, 0),
            (t, high, right, 1),
            (t, low, left, 1),
            (left, low, right, 2),
            (right, high, left, 2),
            (t, whole, sib, 3),
            (left, whole, sib, 3),
            (right, whole, sib, 3),
            (across, low, sib, 3),
            (across, high, sib, 3),
        ]

    def short_routes(first, count):
        whole = pl.ds(first, count)
        return [
            (t, whole, right, 0),
            (t, whole, left, 0),
            (t, whole, across, 1),
            (t, whole, sib, 3),
            (left, whole, sib, 3),
            (right, whole, sib, 3),
            (across, whole, sib, 3),
        ]

    class Gather:
        def __init__(self, buf, own, ss, rs, slot, b, first, count, routes):
            self.buf, self.own, self.slot = buf, own, slot
            self.ss, self.rs = ss, rs
            self.b, self.rows, self.routes = b, pl.ds(first, count), routes

        def send(self, *kinds):
            for kind in kinds:
                source, rows, target, group = self.routes[kind]
                dst = self.buf.at[source, self.b, rows]
                src = dst
                if self.own is not None and source is t:
                    src = self.own.at[self.b, rows]
                remote(
                    src, dst, self.ss.at[self.slot], self.rs.at[group, self.slot], tensor=target
                ).start()

        def blocks(self, count, group):
            ref = self.buf.at[pl.ds(0, count), self.b, self.rows]
            return remote(
                ref, ref, self.ss.at[self.slot], self.rs.at[group, self.slot], tensor=sib
            )

        def arrived(self, group, count=1):
            self.blocks(count, group).wait_recv()

        def sent(self):
            self.blocks(7, 0).wait_send()

        def spread(self):
            for d in range(1, T):
                ref = self.buf.at[t, self.b, self.rows]
                remote(
                    ref,
                    ref,
                    self.ss.at[self.slot],
                    self.rs.at[3, self.slot],
                    tensor=lax.rem(t + d, T),
                ).start()

    def dy(b):
        return Gather(dyf, dy_h, dy_ss, dy_rs, b, b, 0, LEN, ring_routes(0, LEN))

    def dv(b):
        return Gather(dvf, None, dv_ss, dv_rs, b, b, 0, LEN, short_routes(0, LEN))

    dy_hi = Gather(dyf, dy_h, dy_ss, dy_rs, LAST, LAST, LOW, REST, ring_routes(LOW, REST))
    dy_lo = Gather(dyf, dy_h, dy_ss, dy_rs, SEQS, LAST, 0, LOW, short_routes(0, LOW))
    dv_hi = Gather(dvf, None, dv_ss, dv_rs, LAST, LAST, LOW, REST, short_routes(LOW, REST))
    dv_lo = Gather(dvf, None, dv_ss, dv_rs, SEQS, LAST, 0, LOW, short_routes(0, LOW))
    fv = Gather(fvof, None, fv_ss, fv_rs, 0, 0, E, E, short_routes(E, E))
    own_kinds = (0, 1, 2, 3, 6)
    short_kinds = (2, 0, 1, 3)

    def to_peers(src, dst, ss, rs):
        for d in range(1, T):
            remote(src, dst, ss, rs, tensor=lax.rem(t + d, T)).start()

    def both(ref, ss, rs):
        return remote(ref, ref, ss, rs, tensor=sib)

    def e_copy(phase):
        return remote(
            ev.at[0], ev.at[1 + phase], e_ss.at[phase], e_rs.at[phase], section=partner(phase)
        )

    def ps_copy():
        return remote(p_part.at[1 - core], p_sib, xs.at[0], xs.at[1], tensor=sib)

    def dx_copy(b, rows):
        return remote(
            dx_v.at[b, rows],
            gn_h.at[b, rows],
            xs.at[2],
            xs.at[3],
            section=lax.rem(s + nsec - 1, nsec),
        )

    zero = pltpu.make_async_copy(zero_v, gn_h, lsem.at[13])

    def start_eig(phase):
        @pl.when(lax.rem(s // 2**phase, 2) == 0)
        def _():
            pl.semaphore_wait(hello.at[phase], 1)

        e_copy(phase).start()

    def fold_eig(phase):
        e_copy(phase).wait()
        ev[0] = ev[0] + ev[1 + phase]

    dy(0).send(*own_kinds)
    dy(1).send(*own_kinds)

    loads[7].wait()
    ev[0] = jnp.full((1, 128), jnp.sum(eig_v[0] + eig_v[1]), F32)

    for at in (0, 1, 2, 3, 4, 5, 6):
        loads[at].wait()

    def project(b, carry):
        xf = x_v[b].astype(F32)
        scaled = (xf * g_v[...]).astype(BF16)
        sqt[t, b] = jnp.sum(lanes_folded(xf * xf).T, axis=0, keepdims=True)
        part = contract(fo_v[...], ao_v[b])
        part += contract(fs_v[...], dyf[t, b])
        part += contract(fp_v[...], scaled)
        p_part[lax.rem(b, 2), b // 2] = part
        return carry

    lax.fori_loop(0, SEQS, project, 0)
    to_peers(sqt.at[t], sqt.at[t], xs.at[4], xs.at[5])
    ps_copy().start()

    @pl.when(s == nsec - 1)
    def _():
        zero_v[...] = jnp.zeros_like(zero_v)
        zero.start()

    def value_grad(b):
        dy(b).arrived(3, 4)
        acc = contract(wo_v[:, 0:W], dyf[0, b])
        for k in range(1, T):
            acc += contract(wo_v[:, k * W : (k + 1) * W], dyf[k, b])
        d_att = acc.astype(BF16)
        d_att = jnp.concatenate([d_att[h * HD : (h + 1) * HD] for h in range(4)], axis=1)
        probs = aw_v[b].reshape(4 * LEN, LEN)
        d_val = jnp.dot(d_att, probs, preferred_element_type=F32).T
        dvf[t, b] = d_val.astype(BF16)
        dv(b).send(*short_kinds)

    def part_terms(first, count, probs):
        rows = pl.ds(first, count)
        acc = contract(dyf[0, LAST, rows], wo_v[:, 0:W])
        for k in range(1, T):
            acc += contract(dyf[k, LAST, rows], wo_v[:, k * W : (k + 1) * W])
        d_att = acc.astype(BF16)
        d_att = jnp.concatenate([d_att[:, h * HD : (h + 1) * HD] for h in range(4)], axis=0)
        return jnp.dot(probs, d_att, preferred_element_type=F32)

    def input_grad(slot, b, first, count):
        rows = pl.ds(first, count)
        vals = jnp.concatenate([dvf[k, b, rows] for k in range(T)], axis=1)
        du = contract(vals, wv_v[...])
        du_v[b, rows] = du
        cross = lanes_folded(x_v[b, rows].astype(F32) * g_v[...] * du)
        if count < LEN:
            cross = jnp.concatenate([cross, jnp.zeros((LEN - count, 128), F32)], axis=0)
        mb[slot, t] = jnp.sum(cross.T, axis=0, keepdims=True)
        to_peers(mb.at[slot, t], mb.at[slot, t], m_ss.at[slot], m_rs.at[slot])

    def relay(slot, b, first, count):
        rows = pl.ds(first, count)
        both(mb.at[slot, pl.ds(0, T - 1)], m_ss.at[slot], m_rs.at[slot]).wait_recv()
        total = mb[slot, 0]
        for k in range(1, T):
            total += mb[slot, k]
        mean = jnp.broadcast_to(total * (1.0 / D), (LEN, 128)).T[0:count]
        inv = rb[b, rows]
        cubed = inv * inv * inv * mean
        for k in range(4):
            cols = slice(k * 128, (k + 1) * 128)
            dx = (
                dyf[t, b, rows, cols].astype(F32)
                + inv * g_v[:, cols] * du_v[b, rows, cols]
                - x_v[b, rows, cols].astype(F32) * cubed
            )
            dx_v[b, rows, cols] = dx.astype(BF16)

        @pl.when(s > 0)
        def _():
            dx_copy(b, rows).start()

    def share_vals(gather):
        gather.arrived(0, 2)
        gather.send(4, 5)
        gather.arrived(1)
        gather.send(6)

    def step(i, carry):
        dy(i).arrived(0)
        dy(i).send(4, 5)

        @pl.when(i >= 1)
        def _():
            dy(i - 1).arrived(2)
            dy(i - 1).send(9, 10)

        dy(i).arrived(1)
        dy(i).send(7, 8)

        @pl.when(i >= 3)
        def _():
            dv(i - 3).arrived(3, 4)
            input_grad(i - 3, i - 3, 0, LEN)

        for phase in range(phases):

            @pl.when(i == phase)
            def _():
                if phase > 0:
                    fold_eig(phase - 1)
                start_eig(phase)

        @pl.when(i == 1)
        def _():
            for at in (8, 9, 10, 11, 12):
                loads[at].wait()
            fv.send(*short_kinds)
            ps_copy().wait_recv()
            for k in range(3):
                p_snd[k] = p_part[core, k] + p_sib[k]

        @pl.when(i >= 1)
        def _():
            value_grad(i - 1)

        @pl.when(i + 2 < LAST)
        def _():
            dy(i + 2).send(*own_kinds)

        @pl.when(i + 2 == LAST)
        def _():
            dy_hi.send(*own_kinds)

        @pl.when(i + 1 == LAST)
        def _():
            dy_lo.send(0, 1, 2, 3)

        @pl.when(i == 2)
        def _():
            both(sqt.at[pl.ds(0, T - 1)], xs.at[4], xs.at[5]).wait_recv()

            def turn(b, carry):
                total = sqt[0, b]
                for k in range(1, T):
                    total += sqt[k, b]
                inv = lax.rsqrt(total * (1.0 / D) + 1e-05)
                rb[b] = jnp.broadcast_to(inv, (LEN, 128)).T
                return carry

            lax.fori_loop(0, SEQS, turn, 0)
            aw_hi[...] = aw_v[LAST, :, LOW:LEN].reshape(4 * REST, LEN).T
            aw_lo[...] = aw_v[LAST, :, 0:LOW].reshape(4 * LOW, LEN).T

        @pl.when(i >= 2)
        def _():
            share_vals(dv(i - 2))

        @pl.when(i >= 3)
        def _():
            relay(i - 3, i - 3, 0, LEN)

        return carry

    lax.fori_loop(0, LAST, step, 0)

    dy_hi.arrived(0)
    dy_hi.send(4, 5)
    dy(LAST - 1).arrived(2)
    dy(LAST - 1).send(9, 10)
    dy_hi.arrived(1)
    dy_hi.send(7, 8)
    dv(LAST - 3).arrived(3, 4)
    input_grad(LAST - 3, LAST - 3, 0, LEN)
    value_grad(LAST - 1)

    dy_lo.arrived(0, 2)
    dy_lo.send(4, 5)
    dy_hi.arrived(2)
    dy_hi.send(9, 10)
    share_vals(dv(LAST - 2))
    dy_lo.arrived(1)
    dy_lo.send(6)
    relay(LAST - 3, LAST - 3, 0, LEN)
    share_vals(fv)
    for k in range(3):

        @pl.when(chip != k)
        def _():
            slot = lax.rem(chip + 3 - k, 4)
            remote(
                p_snd.at[k], p_rcv.at[slot], xs.at[8], xs.at[9], tensor=2 * k + core
            ).start()

    dy_hi.arrived(3, 4)
    terms = part_terms(LOW, REST, aw_hi[...])
    rest_v[...] = terms[0:LOW]
    dvf[t, LAST, pl.ds(LOW, REST)] = terms[LOW:LEN].astype(BF16)
    dv_hi.send(*short_kinds)
    dv(LAST - 2).arrived(3, 4)
    input_grad(LAST - 2, LAST - 2, 0, LEN)

    dy_lo.arrived(3, 4)
    terms = part_terms(0, LOW, aw_lo[0:LOW])
    dvf[t, LAST, pl.ds(0, LOW)] = (terms + rest_v[...]).astype(BF16)
    dv_lo.send(*short_kinds)

    fold_eig(phases - 1)
    damp = ev[0] * (0.1 / (nsec * 2 * E * E))
    damp = damp[:, 0:E]
    wk[...] = jnp.zeros_like(wk)
    for m in range(2):
        under = eig_v[m] + damp
        for q in range(Q):
            wk[m * 2 * E : m * 2 * E + E, m * 1024 + q * E : m * 1024 + (q + 1) * E] = (
                coef_v[m, q] / under
            )
    row = lax.broadcasted_iota(jnp.int32, (E, W), 0)
    col = lax.broadcasted_iota(jnp.int32, (E, W), 1)
    wk[E : 2 * E, W : 2 * W] = (lax.rem(col, E) == row).astype(F32)

    share_vals(dv(LAST - 1))
    share_vals(dv_hi)
    relay(LAST - 2, LAST - 2, 0, LEN)
    dv(LAST - 1).arrived(3, 4)
    input_grad(LAST - 1, LAST - 1, 0, LEN)
    share_vals(dv_lo)
    dv_hi.arrived(3, 4)
    input_grad(LAST, LAST, LOW, REST)
    dv_lo.arrived(3, 4)
    input_grad(SEQS, LAST, 0, LOW)
    relay(LAST - 1, LAST - 1, 0, LEN)
    relay(LAST, LAST, LOW, REST)
    relay(SEQS, LAST, 0, LOW)

    fv.arrived(3, 4)
    here = sc_h.at[:, pl.ds(pl.multiple_of(t * LEN, LEN), LEN)]
    keep = pltpu.make_async_copy(sc_v, here, lsem.at[14])

    @pl.when(t < SEQS)
    def _():
        both(p_rcv.at[pl.ds(0, 3)], xs.at[8], xs.at[9]).wait_recv()
        proj = p_snd[chip] + p_rcv[0] + p_rcv[1] + p_rcv[2]
        s_val = contract(dvf[0, t], fvof[0, 0])
        for k in range(1, T):
            s_val += contract(dvf[k, t], fvof[k, 0])
        pick = wk[:, W : 2 * W]

        def exact(left, right):
            return jnp.dot(left, right, precision=HIGH, preferred_element_type=F32)

        def exact_turned(left, right):
            return lax.dot_general(
                left, right, (((0,), (0,)), ((), ())), precision=HIGH, preferred_element_type=F32
            )

        rows = slice(0, 3 * E)
        pairs = exact_turned(proj, wk[rows, 0:W]) * exact_turned(proj, wk[rows, W : 2 * W])
        proj = proj * rb[t].T[rows]
        pairs += exact_turned(proj, wk[rows, 2 * W : 3 * W]) * exact(s_val, pick)
        row = lax.broadcasted_iota(jnp.int32, (Q, W), 0)
        col = lax.broadcasted_iota(jnp.int32, (Q, W), 1)
        group = (row == col // E).astype(F32)
        sc_v[...] = lax.dot_general(
            group, pairs, (((1,), (1,)), ((), ())), precision=HIGH, preferred_element_type=F32
        )
        keep.start()
        to_peers(sc_v, here, xs.at[10], xs.at[11])

    def drain(b, carry):
        dy(b).sent()
        dv(b).sent()
        return carry

    def drain_sums(slot, carry):
        both(mb.at[slot, pl.ds(0, T - 1)], m_ss.at[slot], m_rs.at[slot]).wait_send()
        return carry

    lax.fori_loop(0, LAST, drain, 0)
    lax.fori_loop(0, SLOTS, drain_sums, 0)
    for gather in (dy_hi, dy_lo, dv_hi, dv_lo):
        gather.sent()
    both(sqt.at[pl.ds(0, T - 1)], xs.at[4], xs.at[5]).wait_send()
    fv.sent()
    ps_copy().wait_send()

    @pl.when(chip == 3)
    def _():
        both(p_snd.at[pl.ds(0, 3)], xs.at[8], xs.at[9]).wait_send()

    @pl.when(chip < 3)
    def _():
        both(p_snd.at[pl.ds(0, 2)], xs.at[8], xs.at[9]).wait_send()

    @pl.when(s > 0)
    def _():
        both(dx_v, xs.at[2], xs.at[3]).wait_send()

    @pl.when(s < nsec - 1)
    def _():
        both(gn_h, xs.at[2], xs.at[3]).wait_recv()

    @pl.when(s == nsec - 1)
    def _():
        zero.wait()

    @pl.when(t < SEQS)
    def _():
        keep.wait()
        both(wk.at[pl.ds(0, Q), pl.ds(0, 7 * LEN)], xs.at[10], xs.at[11]).wait_send()
        both(sc_h.at[:, pl.ds(0, (SEQS - 1) * LEN)], xs.at[10], xs.at[11]).wait_recv()

    @pl.when(t >= SEQS)
    def _():
        both(sc_h, xs.at[10], xs.at[11]).wait_recv()


def hand_over(gn_h, sc_h, gn_o, sc_o, gn_v, sc_v, in_sem, out_sem):
    pieces = [(gn_h.at[b], gn_v.at[b], gn_o.at[b]) for b in range(SEQS)]
    pieces.append((sc_h, sc_v, sc_o))
    inward = [
        pltpu.make_async_copy(src, mid, in_sem.at[k]) for k, (src, mid, dst) in enumerate(pieces)
    ]
    outward = [
        pltpu.make_async_copy(mid, dst, out_sem.at[k]) for k, (src, mid, dst) in enumerate(pieces)
    ]
    for copy in inward:
        copy.start()
    for first, second in zip(inward, outward):
        first.wait()
        second.start()
    for copy in outward:
        copy.wait()


def per_device(nsec, *arrays):
    (dy, x, g, aw, ao, wv, wo, foi, foo, fvi, fvo, coef, eig) = arrays
    blocks = (SEQS, LEN, W)
    phases = nsec.bit_length() - 1
    dma = pltpu.SemaphoreType.DMA
    vmem = pltpu.VMEM
    grad_next, scores = pl.pallas_call(
        functools.partial(kernel, nsec),
        out_shape=(
            jax.ShapeDtypeStruct(blocks, BF16),
            jax.ShapeDtypeStruct((Q, SEQS * LEN), F32),
        ),
        in_specs=[pl.BlockSpec(memory_space=pltpu.HBM)] * 13,
        out_specs=(pl.BlockSpec(memory_space=pl.ANY), pl.BlockSpec(memory_space=pl.ANY)),
        scratch_shapes=[
            vmem((T, *blocks), BF16),
            vmem((T, SEQS, LEN, HD), BF16),
            vmem(blocks, BF16),
            vmem(blocks, BF16),
            vmem((SEQS, 4, LEN, LEN), BF16),
            vmem((W, 2 * W), BF16),
            vmem((W, D), BF16),
            vmem((3 * E, W), BF16),
            vmem((3 * E, W), BF16),
            vmem((3 * E, W), BF16),
            vmem((T, 1, 128, HD), BF16),
            vmem((1, W), F32),
            vmem((2, Q, E, E), F32),
            vmem((2, E, E), F32),
            vmem(blocks, F32),
            vmem(blocks, BF16),
            vmem((2, 3, 3 * E, LEN), F32),
            vmem((3, 3 * E, LEN), F32),
            vmem((3, 3 * E, LEN), F32),
            vmem((3, 3 * E, LEN), F32),
            vmem((T, SEQS, 1, 128), F32),
            vmem((SEQS, LEN, 128), F32),
            vmem((SLOTS, T, 1, 128), F32),
            vmem((1 + phases, 1, 128), F32),
            vmem((128, 3 * W), F32),
            vmem((Q, LEN), F32),
            vmem(blocks, BF16),
            vmem((LEN, 4 * REST), BF16),
            vmem((LEN, 4 * LOW), BF16),
            vmem((LOW, HD), F32),
            pltpu.SemaphoreType.REGULAR((phases,)),
            dma((15,)),
            dma((SLOTS,)),
            dma((4, SLOTS)),
            dma((SLOTS,)),
            dma((4, SLOTS)),
            dma((SLOTS,)),
            dma((SLOTS,)),
            dma((phases,)),
            dma((phases,)),
            dma((1,)),
            dma((4, 1)),
            dma((12,)),
        ],
        compiler_params=pltpu.CompilerParams(
            collective_id=0, has_side_effects=True, vmem_limit_bytes=LIMIT
        ),
        cost_estimate=pl.CostEstimate(
            flops=8 * 10**9, bytes_accessed=10 * 2**20, transcendentals=0
        ),
    )(
        dy.reshape(blocks),
        x.reshape(blocks),
        g,
        aw,
        ao.reshape(blocks),
        wv,
        wo,
        foi,
        foo,
        fvi,
        fvo,
        coef,
        eig,
    )
    grad_next, scores = pl.pallas_call(
        hand_over,
        out_shape=(
            jax.ShapeDtypeStruct(blocks, BF16),
            jax.ShapeDtypeStruct((Q, SEQS * LEN), F32),
        ),
        in_specs=[pl.BlockSpec(memory_space=pl.ANY)] * 2,
        out_specs=(pl.BlockSpec(memory_space=pl.ANY), pl.BlockSpec(memory_space=pl.ANY)),
        scratch_shapes=[
            vmem(blocks, BF16),
            vmem((Q, SEQS * LEN), F32),
            dma((SEQS + 1,)),
            dma((SEQS + 1,)),
        ],
        compiler_params=pltpu.CompilerParams(vmem_limit_bytes=LIMIT),
    )(grad_next, scores)
    return grad_next.reshape(SEQS * LEN, W), scores.T


def solution(mesh):
    nsec = mesh.shape["section"]
    placed = (
        P("section", "tensor"),
        P("section", "tensor"),
        P("section", "tensor"),
        P("section", None, "tensor", None, None),
        P("section", "tensor"),
        P(("section", "tensor"), None),
        P(("section", "tensor"), None),
        P("section", None, "tensor"),
        P("section", None, "tensor"),
        P("section", None, "tensor"),
        P("section", None, "tensor"),
        P("section", None, None, None, None),
        P("section", None, None, None),
    )
    return jax.shard_map(
        functools.partial(per_device, nsec),
        mesh=mesh,
        in_specs=placed,
        out_specs=(P("section", "tensor"), P("section", None)),
        check_vma=False,
    )
```
